32 devices in a mesh: grp: 2 (over y), seq: 4 (over z), head: 2 (over x), rep: 2 (over core).
Axes of the slice: x: 2, y: 2, z: 4, core: 2. Of those that a mesh axis runs over, the one named last changes fastest.
Arguments:
- events: bfloat16 [8192, 512], P(('grp', 'seq', 'rep')), parts along dimension 0, may hold values from -6 to 6
- norm_gain: float32 [512], replicated, may hold values from 0.1 to 1.9
- in_weight: bfloat16 [512, 4, 512], P(None, None, 'head'), may hold values from -0.25 to 0.25
- out_weight: bfloat16 [512, 512], P('head'), may hold values from -0.25 to 0.25
- pair_mask: int32 [16, 4], P(('grp', 'seq', 'rep')), parts along dimension 0, may hold values from 0 to 1, as said below
- cotangent: bfloat16 [8192, 512], P(('grp', 'seq', 'rep')), parts along dimension 0, may hold values from -6 to 6
Outputs:
- output: bfloat16 [8192, 512], P(('grp', 'seq', 'rep')), parts along dimension 0
- grad_events: float32 [8192, 512], P(('grp', 'seq', 'rep')), parts along dimension 0
- grad_in: float32 [1024, 4, 512], P('grp', None, 'head'), parts along dimension 0
- grad_out: float32 [1024, 512], P(('grp', 'head')), parts along dimension 0
- grad_gain: float32 [1024], P('grp'), parts along dimension 0
The draws below stay inside these ranges and needn't reach their ends.
There are 2 independent parts, one for each index of `grp`. The reference program is written for one: setup_inputs(seed, part) draws one part's arguments, and reference() takes and returns one part's arrays. A program takes and returns all parts, laid end to end along the dimension named above; an argument that names none is the same for every part. Nothing has to cross between parts.
Inputs may be any that keep to these rules, and one draw needn't show every extreme that they name: pair_mask[i, r] is 1 where query block i attends key block i + o_r with o = (-2, -1, 1, 2), else 0; it is 0 wherever i + o_r lies outside the 8 blocks.
All inputs are finite; a program needn't handle non-finite values.
Results may differ from the reference program's by a relative error of at most 0.0072.
Values may be sent and summed in bfloat16 or wider, within the bound.
No kernel may reach another device: no remote copies, remote signals or barrier semaphores. Data moves between devices by JAX's collectives and lax.ppermute only.
A program may use at most 64 MiB of HBM per device.

```python
import jax
import jax.numpy as jnp
from jax import lax

D = 512
H = 8
E = 64
BLOCK = 512
HD = 512
BLOCKS = 8
TOKENS = 4096


def draw_pair_mask(key, part):
    key = jax.random.fold_in(key, 11)
    level_key, entry_key = jax.random.split(key)
    levels = jax.random.randint(level_key, (BLOCKS // 4, 1), 0, 5)
    levels = jnp.repeat(levels, 4, axis=0)
    entries = jax.random.randint(entry_key, (BLOCKS, 4), 0, 4)
    partner_ids = jnp.arange(BLOCKS, dtype=jnp.int32)[:, None] + jnp.array([-2, -1, 1, 2], dtype=jnp.int32)[None, :]
    inside = (partner_ids >= 0) & (partner_ids < BLOCKS)
    return jnp.where(inside & (entries < levels), 1, 0).astype(jnp.int32)


def shard_levels(key, shape, shards, least, largest):
    level, own = 1.0, jax.random.fold_in(key, 6)
    for axis_at, shards_of in shards:
        draws = jnp.exp(jax.random.uniform(jax.random.fold_in(own, axis_at), (shards_of,), jnp.float32, least / len(shards), largest / len(shards)))
        level = level * jnp.repeat(draws, shape[axis_at] // shards_of).reshape([-1 if axis == axis_at else 1 for axis in range(len(shape))])
    return level


def centred(key, shape, deviation, limit, cuts=(), kind=jnp.bfloat16):
    drawn = jax.random.normal(key, shape, jnp.float32) * deviation
    if len(cuts) > 0:
        drawn = shard_levels(key, shape, cuts, -0.22, 0.18) * drawn
    return jnp.clip(drawn, min=-limit, max=limit).astype(kind)


def setup_inputs(seed: int = 0, part: int = 0) -> dict:
    key_of = jax.random.split(jax.random.key(seed), 7)
    own_keys = jax.random.split(jax.random.fold_in(key_of[6], part), 7)
    return {
        "events": centred(own_keys[0], (TOKENS, D), 1.0, 6.0, ((0, 8),)),
        "norm_gain": jnp.clip(1.0 + 0.18 * jax.random.normal(key_of[1], (D,), jnp.float32), 0.1, 1.9),
        "in_weight": centred(key_of[2], (D, 4, HD), D ** -0.5, 0.25, ((2, 2),)),
        "out_weight": centred(key_of[3], (HD, D), HD ** -0.5, 0.25, ((0, 2),)),
        "pair_mask": draw_pair_mask(jax.random.fold_in(jax.random.fold_in(key_of[6], part), 71), part),
        "cotangent": centred(own_keys[5], (TOKENS, D), 1.0, 6.0, ((0, 8),)),
    }


OFFSETS = (-2, -1, 1, 2)

def silu_slope(pre_act):
    sigmoid_part = jax.nn.sigmoid(pre_act)
    return sigmoid_part * (1.0 + pre_act * (1.0 - sigmoid_part))

def pair_scores(queries, keys):
    scores = jnp.einsum('qhe,khe->hqk', queries.astype(jnp.float32), keys.astype(jnp.float32))
    weights = (jax.nn.silu(scores) / BLOCK).astype(jnp.bfloat16)
    return (scores, weights)

def pair_forward(operands):
    queries, keys, values = operands
    scores, weights = pair_scores(queries, keys)
    return jnp.einsum('hqk,khe->qhe', weights.astype(jnp.float32), values.astype(jnp.float32))

def pair_backward(operands):
    queries, keys, values, grad_attn = operands
    scores, weights = pair_scores(queries, keys)
    grad_weights = jnp.einsum('qhe,khe->hqk', grad_attn.astype(jnp.float32), values.astype(jnp.float32))
    grad_scores = (grad_weights * silu_slope(scores) * (1.0 / BLOCK)).astype(jnp.bfloat16)
    scores_float = grad_scores.astype(jnp.float32)
    grad_query = jnp.einsum('hqk,khe->qhe', scores_float, keys.astype(jnp.float32))
    grad_key = jnp.einsum('hqk,qhe->khe', scores_float, queries.astype(jnp.float32))
    grad_value = jnp.einsum('hqk,qhe->khe', weights.astype(jnp.float32), grad_attn.astype(jnp.float32))
    return (grad_query, jnp.stack([grad_key, grad_value], axis=1))

def reference(events, norm_gain, in_weight, out_weight, pair_mask, cotangent):
    token_count = events.shape[0]
    block_count = token_count // BLOCK
    block_ids = jnp.arange(block_count, dtype=jnp.int32)

    def partner(array, offset):
        return jnp.take(array, jnp.clip(block_ids + offset, 0, block_count - 1).astype(jnp.int32), axis=0)

    def send_back(array, offset):
        source = block_ids - offset
        valid = ((source >= 0) & (source < block_count)).astype(jnp.float32)
        taken = jnp.take(array, jnp.clip(source, 0, block_count - 1).astype(jnp.int32), axis=0)
        return taken * valid.reshape((block_count,) + (1,) * (array.ndim - 1))
    x_float = events.astype(jnp.float32)
    inverse = lax.rsqrt(lax.optimization_barrier(jnp.mean(x_float * x_float, axis=1, keepdims=True)) + 1e-06)
    normed = (x_float * inverse * norm_gain).astype(jnp.bfloat16)
    flat_in = in_weight.reshape(D, 4 * HD)
    pre_act = jnp.dot(normed, flat_in, preferred_element_type=jnp.float32)
    acts = jax.nn.silu(pre_act).astype(jnp.bfloat16).reshape(block_count, BLOCK, 4, H, E)
    gate_float = acts[:, :, 0].astype(jnp.float32)
    queries = acts[:, :, 1]
    keys = acts[:, :, 2]
    values = acts[:, :, 3]
    mask_float = pair_mask.astype(jnp.float32)
    attended = lax.map(pair_forward, (queries, keys, values))
    for position, offset in enumerate(OFFSETS):
        term = lax.map(pair_forward, (queries, partner(keys, offset), partner(values, offset)))
        attended = attended + mask_float[:, position][:, None, None, None] * term
    mixed = (attended * gate_float).astype(jnp.bfloat16).reshape(token_count, HD)
    output = jnp.dot(mixed, out_weight, preferred_element_type=jnp.float32).astype(jnp.bfloat16)
    grad_out = jnp.dot(mixed.T, cotangent, preferred_element_type=jnp.float32)
    grad_mixed = jnp.dot(cotangent, out_weight.T, preferred_element_type=jnp.float32).reshape(block_count, BLOCK, H, E)
    grad_attn = (grad_mixed * gate_float).astype(jnp.bfloat16)
    grad_gate = grad_mixed * attended
    grad_query, grad_pair = lax.map(pair_backward, (queries, keys, values, grad_attn))
    for position, offset in enumerate(OFFSETS):
        query_term, pair_term = lax.map(pair_backward, (queries, partner(keys, offset), partner(values, offset), grad_attn))
        weight_mask = mask_float[:, position]
        grad_query = grad_query + weight_mask[:, None, None, None] * query_term
        grad_pair = grad_pair + send_back(weight_mask[:, None, None, None, None] * pair_term, offset)
    grad_stack = jnp.stack([grad_gate, grad_query, grad_pair[:, :, 0], grad_pair[:, :, 1]], axis=2)
    grad_pre = (grad_stack.reshape(token_count, 4 * HD) * silu_slope(pre_act)).astype(jnp.bfloat16)
    grad_in = jnp.dot(normed.T, grad_pre, preferred_element_type=jnp.float32).reshape(D, 4, HD)
    grad_normed = jnp.dot(grad_pre, flat_in.T, preferred_element_type=jnp.float32)
    scaled = grad_normed * norm_gain
    grad_gain = lax.optimization_barrier(jnp.sum(grad_normed * x_float * inverse, axis=0))
    grad_events = inverse * scaled - x_float * (inverse * inverse * inverse) * lax.optimization_barrier(jnp.mean(scaled * x_float, axis=1, keepdims=True))
    return (output, grad_events, grad_in, grad_out, grad_gain)
```

```python
import functools

import jax
import jax.numpy as jnp
from jax import lax
from jax.experimental import pallas as pl
from jax.experimental.pallas import tpu as pltpu
from jax.sharding import PartitionSpec as P

D = 512
E = 64
BLOCK = 512
CHUNKS = 4
F32 = jnp.float32
BF16 = jnp.bfloat16
VMEM_BYTES = 40 * 1024 * 1024


def dot_nt(a, b):
    return lax.dot_general(a, b, (((1,), (1,)), ((), ())), preferred_element_type=F32)


def dot_tn(a, b):
    return lax.dot_general(a, b, (((0,), (0,)), ((), ())), preferred_element_type=F32)


def dot_nn(a, b):
    return lax.dot_general(a, b, (((1,), (0,)), ((), ())), preferred_element_type=F32)


def sigmoid(x):
    return 0.5 * jnp.tanh(0.5 * x) + 0.5


def silu_slope(x):
    s = sigmoid(x)
    return s * (1.0 + x * (1.0 - s))


def whole(shape):
    zeros = (0,) * len(shape)
    return pl.BlockSpec(shape, lambda *_: zeros)


def call(kernel, out_shapes, args, scalars=(), flops=0, trans=0):
    size = sum(a.size * a.dtype.itemsize for a in args)
    size += sum(o.size * o.dtype.itemsize for o in out_shapes)
    return pl.pallas_call(
        kernel,
        out_shape=out_shapes,
        in_specs=[pl.BlockSpec(memory_space=pltpu.SMEM)] * len(scalars)
        + [pl.BlockSpec(memory_space=pltpu.VMEM)] * len(args),
        out_specs=[pl.BlockSpec(memory_space=pltpu.VMEM)] * len(out_shapes),
        compiler_params=pltpu.CompilerParams(vmem_limit_bytes=VMEM_BYTES),
        cost_estimate=pl.CostEstimate(flops=flops, bytes_accessed=size, transcendentals=trans),
    )(*scalars, *args)


def shape(dims, dtype):
    return jax.ShapeDtypeStruct(dims, dtype)


def project_kv_kernel(own_slot, ev_own, ev_oth, gain, w_kv, normed, pre, kv):
    for slot in range(2):
        rows = pl.ds(slot * BLOCK, BLOCK)
        mine = own_slot[0] == slot
        x = jnp.where(mine, ev_own[...].astype(F32), ev_oth[...].astype(F32))
        inverse = lax.rsqrt(jnp.mean(x * x, axis=1, keepdims=True) + 1e-06)
        n = (x * inverse * gain[...]).astype(BF16)
        normed[rows, :] = n
        p = dot_nn(n, w_kv[...])
        pre[rows, :] = p
        kv[rows, :] = (p * sigmoid(p)).astype(BF16)


def project_gq_kernel(own_slot, cot_own, cot_oth, w_gq, wow, normed, pre, qa, gate, gm):
    w = wow.shape[0]
    for slot in range(2):
        rows = pl.ds(slot * BLOCK, BLOCK)
        mine = own_slot[0] == slot
        cot = jnp.where(mine, cot_own[...].astype(F32), cot_oth[...].astype(F32)).astype(BF16)
        p = dot_nn(normed[rows, :], w_gq[...])
        pre[rows, :] = p
        act = (p * sigmoid(p)).astype(BF16)
        g = act[:, :w]
        gate[rows, :] = g
        grad_mixed = dot_nt(cot, wow[...])
        gm[rows, :] = grad_mixed
        qa[rows, :w] = act[:, w:]
        qa[rows, w:] = (grad_mixed * g.astype(F32)).astype(BF16)


TILE = 256


def pair_side(left, p_slot, right, r_slot, acc):
    w = left.shape[1] // 2
    r_rows = pl.ds(r_slot * BLOCK, BLOCK)
    xr, yr = right[r_rows, :w], right[r_rows, w:]
    lane = lax.broadcasted_iota(jnp.int32, (1, w), 1) // E
    zero = jnp.zeros_like(xr)
    heads = []
    for h in range(w // E):
        on = lane == h
        heads.append((jnp.where(on, xr, zero), jnp.where(on, yr, zero)))
    for t in range(BLOCK // TILE):
        rows = pl.ds(p_slot * BLOCK + t * TILE, TILE)
        x = left[rows, :w] * jnp.asarray(0.5, BF16)
        y = left[rows, w:]
        acc_x = acc[rows, :w]
        acc_y = acc[rows, w:]
        for xh, yh in heads:
            u = dot_nt(x, xh)
            g = dot_nt(y, yh)
            a = 1.0 + jnp.tanh(u)
            m = u * a
            slope = a + m * (2.0 - a)
            acc_y = acc_y + dot_nn(m.astype(BF16), yh)
            acc_x = acc_x + dot_nn((g * slope).astype(BF16), xh)
        acc[rows, :w] = acc_x
        acc[rows, w:] = acc_y


def side_kernel(pairs, n_right, mask, left, *rest):
    rights, acc = rest[:n_right], rest[n_right]
    acc[...] = jnp.zeros_like(acc)
    for p_slot, r_arr, r_slot, row, col in pairs:
        run = functools.partial(pair_side, left, p_slot, rights[r_arr], r_slot, acc)
        if row is None:
            run()
        else:
            pl.when(mask[row, col] == 1)(run)


def own_kernel(mask, qa, kv, acc_q, acc_k):
    acc_q[...] = jnp.zeros_like(acc_q)
    acc_k[...] = jnp.zeros_like(acc_k)
    for q_slot, k_slot, col in ((0, 0, None), (1, 1, None), (0, 1, 1), (1, 0, 2)):

        def run():
            pair_side(qa, q_slot, kv, k_slot, acc_q)
            pair_side(kv, k_slot, qa, q_slot, acc_k)

        if col is None:
            run()
        else:
            pl.when(mask[q_slot, col] == 1)(run)


def query_finish_kernel(own_slot, cot_own, cot_oth, gate, gm, pre, normed, *rest):
    accs, (mixed, gp, packed) = rest[:-3], rest[-3:]
    w = gate.shape[1]
    grad_in = jnp.zeros((D, 2 * w), F32)
    grad_out = jnp.zeros((w, D), F32)
    for slot in range(2):
        rows = pl.ds(slot * BLOCK, BLOCK)
        total = accs[0][rows, :]
        for more in accs[1:]:
            total = total + more[rows, :]
        grad_query = total[:, :w] * (1.0 / 1024)
        attended = total[:, w:] * (1.0 / 512)
        mix = (attended * gate[rows, :].astype(F32)).astype(BF16)
        mixed[rows, :] = mix
        slope = silu_slope(pre[rows, :])
        gp_g = (gm[rows, :] * attended * slope[:, :w]).astype(BF16)
        gp_q = (grad_query * slope[:, w:]).astype(BF16)
        gp[rows, :w] = gp_g
        gp[rows, w:] = gp_q
        grad_in = grad_in + dot_tn(normed[rows, :], gp[rows, :])
        mine = own_slot[0] == slot
        cot = jnp.where(mine, cot_own[...].astype(F32), cot_oth[...].astype(F32)).astype(BF16)
        grad_out = grad_out + dot_tn(mix, cot)
    pack(packed, grad_in, grad_out)


def pack(packed, grad_in, grad_out=None):
    step = D // CHUNKS
    width = grad_in.shape[1]
    for c in range(CHUNKS):
        packed[c, :step, :] = grad_in[c * step : (c + 1) * step].astype(BF16)
        if grad_out is not None:
            n = grad_out.shape[0] // CHUNKS
            part = grad_out[c * n : (c + 1) * n].astype(BF16)
            for j in range(D // width):
                packed[c, step + j * n : step + (j + 1) * n, :] = part[:, j * width : (j + 1) * width]


def key_finish_kernel(own_slot, ev_own, ev_oth, pre, normed, gp_gq, w_gq, w_kv, *rest):
    accs, (packed, gn_own, gn_oth, pg) = rest[:-4], rest[-4:]
    w = pre.shape[1] // 2
    grad_in = jnp.zeros((D, 2 * w), F32)
    gain = jnp.zeros((1, D), F32)
    for slot in range(2):
        rows = pl.ds(slot * BLOCK, BLOCK)
        total = accs[0][rows, :]
        for more in accs[1:]:
            total = total + more[rows, :]
        slope = silu_slope(pre[rows, :])
        gp_k = (total[:, :w] * (1.0 / 1024) * slope[:, :w]).astype(BF16)
        gp_v = (total[:, w:] * (1.0 / 512) * slope[:, w:]).astype(BF16)
        gp = jnp.concatenate([gp_k, gp_v], axis=1)
        grad_in = grad_in + dot_tn(normed[rows, :], gp)
        gn = dot_nt(gp_gq[rows, :], w_gq[...]) + dot_nt(gp, w_kv[...])
        mine = own_slot[0] == slot
        x = jnp.where(mine, ev_own[...].astype(F32), ev_oth[...].astype(F32))
        inverse = lax.rsqrt(jnp.mean(x * x, axis=1, keepdims=True) + 1e-06)
        gain = gain + jnp.sum(gn * x * inverse, axis=0, keepdims=True)
        half = gn.astype(BF16)

        @pl.when(mine)
        def _():
            gn_own[...] = half

        @pl.when(jnp.logical_not(mine))
        def _():
            gn_oth[...] = half

    pack(packed, grad_in)
    pg[...] = gain


def events_kernel(events, gain, mine, other, grad):
    x = events[...].astype(F32)
    inverse = lax.rsqrt(jnp.mean(x * x, axis=1, keepdims=True) + 1e-06)
    gn = mine[...].astype(F32) + other[...].astype(F32)
    scaled = gn * gain[...]
    mean = jnp.mean(scaled * x, axis=1, keepdims=True)
    grad[...] = inverse * scaled - x * (inverse * inverse * inverse) * mean


def output_kernel(mine, other, w_mine, w_other, out):
    out[...] = (dot_nn(mine[...], w_mine[...]) + dot_nn(other[...], w_other[...])).astype(BF16)


def swap(x, axis, bit=1):
    n = lax.axis_size(axis)
    return lax.ppermute(x, axis, [(i, i ^ bit) for i in range(n)])


def route_even(n):
    return [(2 * i + r, 2 * (i ^ 1) + r) for i in range(n) for r in range(2)]


def route_odd(n):
    route = []
    for i in range(n):
        for r in range(2):
            if i in (0, n - 1):
                route.append((2 * i + r, 2 * i + 1 - r))
            else:
                route.append((2 * i + r, 2 * (((i - 1) ^ 1) + 1) + r))
    return route


def reduce_over_seq(packed):
    n = lax.axis_size("seq")
    if n != CHUNKS:
        return lax.psum(packed.astype(F32), "seq").astype(BF16)
    me = lax.axis_index("seq")

    def chunk(d):
        return lax.dynamic_index_in_dim(packed, me ^ d, 0, keepdims=False)

    got = [swap(chunk(d), "seq", d) for d in (1, 2, 3)]
    total = (chunk(0).astype(F32) + got[0].astype(F32)) + (got[1].astype(F32) + got[2].astype(F32))
    total = total.astype(BF16)
    parts = [total] + [swap(total, "seq", d) for d in (1, 2, 3)]
    out = jnp.zeros_like(packed)
    for d in range(4):
        out = lax.dynamic_update_index_in_dim(out, parts[d], me ^ d, 0)
    return out


def head_others(x):
    n = lax.axis_size("head")
    if n == 2:
        return swap(x, "head")
    gathered = lax.all_gather(x, "head", axis=0)
    me = lax.axis_index("head")
    keep = jnp.arange(n) != me
    return gathered, keep


def body(events, norm_gain, in_weight, out_weight, pair_mask, cotangent):
    n_seq, n_head = lax.axis_size("seq"), lax.axis_size("head")
    rep, seq = lax.axis_index("rep"), lax.axis_index("seq")
    w = in_weight.shape[2] // 2
    rows2 = 2 * BLOCK
    flip = 1 - seq % 2
    own = rep ^ flip
    own_slot = own.reshape(1).astype(jnp.int32)

    ev_oth = swap(events, "rep")
    cot_oth = swap(cotangent, "rep")
    mask_oth = swap(pair_mask, "rep")
    gain = norm_gain.reshape(1, D)
    w_mine = lax.dynamic_slice(in_weight, (0, 0, rep * w), (D, 4, w))
    w_gq = w_mine[:, 0:2].reshape(D, 2 * w)
    w_kv = w_mine[:, 2:4].reshape(D, 2 * w)
    wow = lax.dynamic_slice(out_weight, (rep * w, 0), (w, D))
    ow_rot = jnp.concatenate(
        [wow, lax.dynamic_slice(out_weight, ((1 - rep) * w, 0), (w, D))], axis=0
    )

    masks = jnp.where(own == 0, jnp.concatenate([pair_mask, mask_oth]), jnp.concatenate([mask_oth, pair_mask]))
    masks = jnp.where(flip == 1, masks, masks[:, ::-1])
    axes = ("seq", "rep")
    even, odd = route_even(n_seq), route_odd(n_seq)
    edge = (seq == 0) | (seq == n_seq - 1)
    mask_even = lax.ppermute(masks, axes, even)
    mask_odd = jnp.where(edge, 0, lax.ppermute(masks, axes, odd))

    normed, pre_kv, kv = call(
        project_kv_kernel,
        [shape((rows2, D), BF16), shape((rows2, 2 * w), F32), shape((rows2, 2 * w), BF16)],
        [events, ev_oth, gain, w_kv],
        [own_slot],
        flops=2 * rows2 * D * 2 * w,
    )
    kv_even = lax.ppermute(kv, axes, even)
    kv_odd = lax.ppermute(kv, axes, odd)
    pre_gq, qa, gate, gm = call(
        project_gq_kernel,
        [shape((rows2, 2 * w), F32), shape((rows2, 2 * w), BF16), shape((rows2, w), BF16), shape((rows2, w), F32)],
        [cotangent, cot_oth, w_gq, wow, normed],
        [own_slot],
        flops=2 * rows2 * D * 3 * w,
    )
    qa_even = lax.ppermute(qa, axes, even)
    qa_odd = lax.ppermute(qa, axes, odd)
    acc_shape = shape((rows2, 2 * w), F32)
    side_flops = 8 * BLOCK * BLOCK * 2 * w
    q_own, k_own = call(own_kernel, [acc_shape] * 2, [qa, kv], [masks], flops=8 * side_flops)

    q_pairs = (
        (0, 0, 0, 0, 2), (1, 0, 0, 1, 3), (0, 0, 1, 0, 3),
        (1, 1, 1, 1, 1), (0, 1, 1, 0, 0), (1, 1, 0, 1, 0),
    )
    (q_far,) = call(
        functools.partial(side_kernel, q_pairs, 2),
        [acc_shape],
        [qa, kv_even, kv_odd],
        [masks],
        flops=6 * side_flops,
    )
    mixed, gp_gq, pack_q = call(
        query_finish_kernel,
        [
            shape((rows2, w), BF16),
            shape((rows2, 2 * w), BF16),
            shape((CHUNKS, D // CHUNKS + w * D // (CHUNKS * 2 * w), 2 * w), BF16),
        ],
        [cotangent, cot_oth, gate, gm, pre_gq, normed, q_own, q_far],
        [own_slot],
        flops=2 * rows2 * D * 3 * w,
    )
    sum_q = reduce_over_seq(pack_q)
    sum_q_oth = swap(sum_q, "rep")

    mix_own = lax.dynamic_slice(mixed, (own * BLOCK, 0), (BLOCK, w))
    mix_send = lax.dynamic_slice(mixed, ((1 - own) * BLOCK, 0), (BLOCK, w))
    mix_blk = jnp.concatenate([mix_own, swap(mix_send, "rep")], axis=1)
    if n_head == 2:
        (output,) = call(
            output_kernel,
            [shape((BLOCK, D), BF16)],
            [mix_blk, swap(mix_blk, "head"), ow_rot, swap(ow_rot, "head")],
            flops=2 * BLOCK * D * D,
        )
    else:
        output = lax.psum(dot_nn(mix_blk, ow_rot), "head").astype(BF16)

    masks_kv = jnp.concatenate([mask_even, mask_odd])
    k_pairs = (
        (0, 0, 0, 0, 2), (0, 0, 1, 1, 3), (1, 0, 0, 0, 3),
        (1, 1, 1, 3, 1), (1, 1, 0, 2, 0), (0, 1, 1, 3, 0),
    )
    (k_far,) = call(
        functools.partial(side_kernel, k_pairs, 2),
        [acc_shape],
        [kv, qa_even, qa_odd],
        [masks_kv],
        flops=6 * side_flops,
    )
    pack_kv, gn_own, gn_oth, pg = call(
        key_finish_kernel,
        [
            shape((CHUNKS, D // CHUNKS, 2 * w), BF16),
            shape((BLOCK, D), BF16),
            shape((BLOCK, D), BF16),
            shape((1, D), F32),
        ],
        [events, ev_oth, pre_kv, normed, gp_gq, w_gq, w_kv, k_own, k_far],
        [own_slot],
        flops=2 * rows2 * D * 6 * w,
    )
    gn_blk = (gn_own.astype(F32) + swap(gn_oth, "rep").astype(F32)).astype(BF16)
    if n_head == 2:
        gn_x = swap(gn_blk, "head")
    else:
        gn_x = lax.psum(gn_blk.astype(F32), "head") - gn_blk.astype(F32)
    sum_kv = reduce_over_seq(pack_kv)
    sum_kv_oth = swap(sum_kv, "rep")
    (grad_events,) = call(
        events_kernel, [shape((BLOCK, D), F32)], [events, gain, gn_blk, gn_x], flops=BLOCK * D * 12
    )
    if n_head == 2 and n_seq == 4:
        pg = pg + swap(pg, "rep")
        pg = pg + swap(pg, "head")
        pg = pg + swap(pg, "seq", 1)
        pg = pg + swap(pg, "seq", 2)
    else:
        pg = lax.psum(pg, ("seq", "head", "rep"))
    grad_gain = pg.reshape(D)

    def unpack(got_q, got_kv):
        step = D // CHUNKS
        gq = got_q[:, :step].reshape(D, 2, w)
        gkv = got_kv.reshape(D, 2, w)
        n = w // CHUNKS
        out = got_q[:, step:].reshape(CHUNKS, D // (2 * w), n, 2 * w)
        out = out.transpose(0, 2, 1, 3).reshape(w, D)
        return jnp.concatenate([gq, gkv], axis=1), out

    in_a, out_a = unpack(sum_q, sum_kv)
    in_b, out_b = unpack(sum_q_oth, sum_kv_oth)
    grad_in = jnp.where(
        rep == 0, jnp.concatenate([in_a, in_b], axis=2), jnp.concatenate([in_b, in_a], axis=2)
    ).astype(F32)
    grad_out = jnp.where(
        rep == 0, jnp.concatenate([out_a, out_b], axis=0), jnp.concatenate([out_b, out_a], axis=0)
    ).astype(F32)
    return (output, grad_events, grad_in, grad_out, grad_gain)


def solution(mesh):
    return jax.shard_map(
        body,
        mesh=mesh,
        in_specs=(
            P(("grp", "seq", "rep"), None),
            P(),
            P(None, None, "head"),
            P("head", None),
            P(("grp", "seq", "rep"), None),
            P(("grp", "seq", "rep"), None),
        ),
        out_specs=(
            P(("grp", "seq", "rep"), None),
            P(("grp", "seq", "rep"), None),
            P("grp", None, "head"),
            P(("grp", "head"), None),
            P("grp"),
        ),
        check_vma=False,
    )
```

```python
import functools

import jax
import jax.numpy as jnp
from jax import lax
from jax.experimental import pallas as pl
from jax.experimental.pallas import tpu as pltpu
from jax.sharding import PartitionSpec as P

D = 512
E = 64
BLOCK = 512
CHUNKS = 4
MASK_ROWS = 16
GAIN_ROWS = 16
F32 = jnp.float32
BF16 = jnp.bfloat16
VMEM_BYTES = 16 * 1024 * 1024


def dot_nt(a, b):
    return lax.dot_general(a, b, (((1,), (1,)), ((), ())), preferred_element_type=F32)


def dot_tn(a, b):
    return lax.dot_general(a, b, (((0,), (0,)), ((), ())), preferred_element_type=F32)


def dot_nn(a, b):
    return lax.dot_general(a, b, (((1,), (0,)), ((), ())), preferred_element_type=F32)


def sigmoid(x):
    return 0.5 * jnp.tanh(0.5 * x) + 0.5


def silu_slope(x):
    s = sigmoid(x)
    return s * (1.0 + x * (1.0 - s))


def whole(shape):
    zeros = (0,) * len(shape)
    return pl.BlockSpec(shape, lambda *_: zeros)


def call(kernel, out_shapes, args, scalars=(), us=1.0, fetched=0):
    size = sum(a.size * a.dtype.itemsize for a in args)
    size += sum(o.size * o.dtype.itemsize for o in out_shapes)
    n_scalars, n_out = len(scalars), len(out_shapes)

    def with_fetch(*refs):
        head, held, rest = refs[:n_scalars], refs[n_scalars : n_scalars + fetched], refs[n_scalars + fetched :]
        n_rest = len(args) - fetched + n_out
        slots, sems = rest[n_rest : n_rest + fetched], rest[n_rest + fetched]
        copies = [pltpu.make_async_copy(h, slot, sems.at[i]) for i, (h, slot) in enumerate(zip(held, slots))]
        for copy in copies:
            copy.start()
        for copy in copies:
            copy.wait()
        kernel(*head, *slots, *rest[:n_rest])

    scratch = [pltpu.VMEM(a.shape, a.dtype) for a in args[:fetched]]
    return pl.pallas_call(
        with_fetch if fetched else kernel,
        out_shape=out_shapes,
        in_specs=[pl.BlockSpec(memory_space=pltpu.SMEM)] * n_scalars
        + [pl.BlockSpec(memory_space=pltpu.HBM)] * fetched
        + [pl.BlockSpec(memory_space=pltpu.VMEM)] * (len(args) - fetched),
        out_specs=[pl.BlockSpec(memory_space=pltpu.VMEM)] * n_out,
        scratch_shapes=scratch + [pltpu.SemaphoreType.DMA((fetched,))] if fetched else [],
        compiler_params=pltpu.CompilerParams(vmem_limit_bytes=VMEM_BYTES),
        cost_estimate=pl.CostEstimate(flops=int(us * 1.1e9), bytes_accessed=size, transcendentals=0),
    )(*scalars, *args)


def shape(dims, dtype):
    return jax.ShapeDtypeStruct(dims, dtype)


def pick(where, slot, own, oth):
    return jnp.where(where[0] == slot, own[...].astype(F32), oth[...].astype(F32))


def mask_at(where, mask_own, mask_oth, slot, col):
    at = jnp.where(where[1] == 1, col, 3 - col)
    return jnp.where(where[0] == slot, mask_own[0, at], mask_oth[0, at])


def project_kv_kernel(where, ev_own, ev_oth, w4, gain, normed, pre, kv):
    w_kv = jnp.concatenate([w4[2], w4[3]], axis=1)
    for slot in range(2):
        rows = pl.ds(slot * BLOCK, BLOCK)
        x = pick(where, slot, ev_own, ev_oth)
        inverse = lax.rsqrt(jnp.mean(x * x, axis=1, keepdims=True) + 1e-06)
        n = (x * inverse * gain[...]).astype(BF16)
        normed[rows, :] = n
        p = dot_nn(n, w_kv)
        pre[rows, :] = p
        kv[rows, :] = (p * sigmoid(p)).astype(BF16)


def project_gq_kernel(where, mask_own, mask_oth, cot_own, cot_oth, w4, ow, normed, pre, qa, gate, gm):
    w = w4.shape[2]
    w_gq = jnp.concatenate([w4[0], w4[1]], axis=1)
    wow = ow[pl.ds(pl.multiple_of(where[3] * w, w), w), :]
    for slot in range(2):
        rows = pl.ds(slot * BLOCK, BLOCK)
        cot = pick(where, slot, cot_own, cot_oth).astype(BF16)
        p = dot_nn(normed[rows, :], w_gq)
        pre[rows, :] = p
        act = (p * sigmoid(p)).astype(BF16)
        g = act[:, :w]
        gate[rows, :] = g
        grad_mixed = dot_nt(cot, wow)
        gm[rows, :] = grad_mixed
        qa[rows, :w] = act[:, w:]
        qa[rows, w:] = (grad_mixed * g.astype(F32)).astype(BF16)
    lane = lax.broadcasted_iota(jnp.int32, (MASK_ROWS, 2 * w), 1)
    marks = jnp.zeros((MASK_ROWS, 2 * w), F32)
    for slot in range(2):
        for col in range(4):
            m = mask_at(where, mask_own, mask_oth, slot, col).astype(F32)
            marks = jnp.where(lane == 4 * slot + col, m, marks)
    qa[2 * BLOCK :, :] = marks.astype(BF16)


TILE = 256


def pair_side(left, p_slot, right, r_slot, acc):
    w = left.shape[1] // 2
    r_rows = pl.ds(r_slot * BLOCK, BLOCK)
    xr, yr = right[r_rows, :w], right[r_rows, w:]
    lane = lax.broadcasted_iota(jnp.int32, (1, w), 1) // E
    zero = jnp.zeros_like(xr)
    heads = []
    for h in range(w // E):
        on = lane == h
        heads.append((jnp.where(on, xr, zero), jnp.where(on, yr, zero)))
    for t in range(BLOCK // TILE):
        rows = pl.ds(p_slot * BLOCK + t * TILE, TILE)
        x = left[rows, :w] * jnp.asarray(0.5, BF16)
        y = left[rows, w:]
        acc_x = acc[rows, :w]
        acc_y = acc[rows, w:]
        for xh, yh in heads:
            u = dot_nt(x, xh)
            g = dot_nt(y, yh)
            a = 1.0 + jnp.tanh(u)
            m = u * a
            slope = a + m * (2.0 - a)
            acc_y = acc_y + dot_nn(m.astype(BF16), yh)
            acc_x = acc_x + dot_nn((g * slope).astype(BF16), xh)
        acc[rows, :w] = acc_x
        acc[rows, w:] = acc_y


OWN_PAIRS = ((0, 0, None), (1, 1, None), (0, 1, 1), (1, 0, 2))
EVEN_PAIRS = ((0, 0, 2), (1, 0, 3), (0, 1, 3))
ODD_PAIRS = ((1, 1, 1), (0, 1, 0), (1, 0, 0))


def query_kernel(where, mask_own, mask_oth, qa, kv_even, kv_odd, acc):
    acc[...] = jnp.zeros_like(acc)
    for kv, pairs in ((kv_even, EVEN_PAIRS), (kv_odd, ODD_PAIRS)):
        for q_slot, k_slot, col in pairs:
            run = functools.partial(pair_side, qa, q_slot, kv, k_slot, acc)
            pl.when(mask_at(where, mask_own, mask_oth, q_slot, col) == 1)(run)


KEY_PAIRS = tuple((0, *pair) for pair in EVEN_PAIRS) + tuple((1, *pair) for pair in ODD_PAIRS)


def key_kernel(pairs, where, kv, qa_even, qa_odd, acc):
    acc[...] = jnp.zeros_like(acc)
    for odd, q_slot, k_slot, col in pairs:
        qa = qa_odd if odd else qa_even
        marks = qa[2 * BLOCK :, :].astype(F32)
        row = lax.broadcasted_iota(jnp.int32, marks.shape, 0)
        lane = lax.broadcasted_iota(jnp.int32, marks.shape, 1)
        m = jnp.sum(jnp.where((row == 0) & (lane == 4 * q_slot + col), marks, 0.0))
        on = m > 0.5
        if odd:
            on = on & (where[2] == 0)
        pl.when(on)(functools.partial(pair_side, kv, k_slot, qa, q_slot, acc))


def own_kernel(where, mask_own, mask_oth, qa, kv, acc_q, acc_k):
    acc_q[...] = jnp.zeros_like(acc_q)
    acc_k[...] = jnp.zeros_like(acc_k)
    for q_slot, k_slot, col in OWN_PAIRS:
        if col is None:
            pair_side(qa, q_slot, kv, k_slot, acc_q)
            pair_side(kv, k_slot, qa, q_slot, acc_k)
        else:
            run = functools.partial(pair_side, qa, q_slot, kv, k_slot, acc_q)
            pl.when(mask_at(where, mask_own, mask_oth, q_slot, col) == 1)(run)


def last_key_kernel(where, mask_own, mask_oth, kv, qa_even, qa_odd, qa, acc):
    key_kernel(KEY_PAIRS[4:], where, kv, qa_even, qa_odd, acc)
    for q_slot, k_slot, col in OWN_PAIRS[2:]:
        run = functools.partial(pair_side, kv, k_slot, qa, q_slot, acc)
        pl.when(mask_at(where, mask_own, mask_oth, q_slot, col) == 1)(run)


def query_finish_kernel(where, cot_own, cot_oth, gate, gm, pre, normed, *rest):
    accs, (mix_own, mix_oth, gp, packed) = rest[:-4], rest[-4:]
    w = gate.shape[1]
    grad_in = jnp.zeros((D, 2 * w), F32)
    grad_out = jnp.zeros((w, D), F32)
    for slot in range(2):
        rows = pl.ds(slot * BLOCK, BLOCK)
        total = accs[0][rows, :]
        for more in accs[1:]:
            total = total + more[rows, :]
        grad_query = total[:, :w] * (1.0 / 1024)
        attended = total[:, w:] * (1.0 / 512)
        mix = (attended * gate[rows, :].astype(F32)).astype(BF16)
        store_by_owner(where, slot, mix, mix_own, mix_oth)
        slope = silu_slope(pre[rows, :])
        gp_g = (gm[rows, :] * attended * slope[:, :w]).astype(BF16)
        gp_q = (grad_query * slope[:, w:]).astype(BF16)
        gp[rows, :w] = gp_g
        gp[rows, w:] = gp_q
        grad_in = grad_in + dot_tn(normed[rows, :], gp[rows, :])
        cot = pick(where, slot, cot_own, cot_oth).astype(BF16)
        grad_out = grad_out + dot_tn(mix, cot)
    pack(packed, grad_in, grad_out)


def store_by_owner(where, slot, value, own, oth):
    @pl.when(where[0] == slot)
    def _():
        own[...] = value

    @pl.when(where[0] != slot)
    def _():
        oth[...] = value


def pack(packed, grad_in, grad_out=None):
    step = D // CHUNKS
    w = grad_in.shape[1] // 2
    for c in range(CHUNKS):
        for p in range(2):
            packed[c, p * step : (p + 1) * step, :] = grad_in[c * step : (c + 1) * step, p * w : (p + 1) * w].astype(BF16)
        if grad_out is not None:
            n = w // CHUNKS
            part = grad_out[c * n : (c + 1) * n].astype(BF16)
            for j in range(D // w):
                packed[c, 2 * step + j * n : 2 * step + (j + 1) * n, :] = part[:, j * w : (j + 1) * w]


def key_finish_kernel(where, ev_own, ev_oth, pre, normed, gp_gq, w4, *rest):
    accs, (packed, gn_own, gn_oth, pg) = rest[:-4], rest[-4:]
    w = pre.shape[1] // 2
    w_gq = jnp.concatenate([w4[0], w4[1]], axis=1)
    w_kv = jnp.concatenate([w4[2], w4[3]], axis=1)
    grad_in = jnp.zeros((D, 2 * w), F32)
    gain = jnp.zeros((1, D), F32)
    for slot in range(2):
        rows = pl.ds(slot * BLOCK, BLOCK)
        total = accs[0][rows, :]
        for more in accs[1:]:
            total = total + more[rows, :]
        slope = silu_slope(pre[rows, :])
        gp_k = (total[:, :w] * (1.0 / 1024) * slope[:, :w]).astype(BF16)
        gp_v = (total[:, w:] * (1.0 / 512) * slope[:, w:]).astype(BF16)
        gp = jnp.concatenate([gp_k, gp_v], axis=1)
        grad_in = grad_in + dot_tn(normed[rows, :], gp)
        gn = dot_nt(gp_gq[rows, :], w_gq) + dot_nt(gp, w_kv)
        x = pick(where, slot, ev_own, ev_oth)
        inverse = lax.rsqrt(jnp.mean(x * x, axis=1, keepdims=True) + 1e-06)
        gain = gain + jnp.sum(gn * x * inverse, axis=0, keepdims=True)
        store_by_owner(where, slot, gn.astype(BF16), gn_own, gn_oth)
    pack(packed, grad_in)
    pg[...] = gain


def add_cores_kernel(a, b, pg_a, pg_b, top, bottom, pg):
    half = a.shape[0] // 2
    total = (a[...].astype(F32) + b[...].astype(F32)).astype(BF16)
    top[...] = total[:half]
    bottom[...] = total[half:]
    pg[...] = pg_a[...] + pg_b[...]


def add_chunks_kernel(*refs):
    pieces, out = refs[:4], refs[4]
    a, b, c, d = (piece[...].astype(F32) for piece in pieces)
    out[...] = ((a + b) + (c + d)).astype(BF16)


def add_chunks_gain_kernel(a, b, c, d, pg_a, pg_b, out):
    n, w = a.shape
    add_chunks_kernel(a, b, c, d, out.at[:n])
    total = pg_a[...] + pg_b[...]
    high = total.astype(BF16).astype(F32)
    parts = [v[:, j * w : (j + 1) * w] for v in (high, total - high) for j in range(D // w)]
    parts.append(jnp.zeros((GAIN_ROWS - len(parts), w), F32))
    out[n:, :] = jnp.concatenate(parts, axis=0).astype(BF16)


def assemble_kernel(has_gain, where, *refs):
    pieces, outs = refs[:16], refs[16:]
    grad_in, grad_out = outs[:2]
    w = pieces[0].shape[1]
    step = D // CHUNKS
    n = w // CHUNKS

    def place(q_pieces, kv_pieces, core):
        lanes = slice(core * w, (core + 1) * w)
        for i in range(4):
            c = where[4 + i]
            rows = pl.ds(pl.multiple_of(c * step, step), step)
            for p in range(2):
                part = slice(p * step, (p + 1) * step)
                grad_in[rows, p, lanes] = q_pieces[i][part, :].astype(F32)
                grad_in[rows, p + 2, lanes] = kv_pieces[i][part, :].astype(F32)
            for j in range(D // w):
                block = q_pieces[i][2 * step + j * n : 2 * step + (j + 1) * n, :]
                out_rows = pl.ds(pl.multiple_of(core * w + c * n, n), n)
                grad_out[out_rows, j * w : (j + 1) * w] = block.astype(F32)

    for core in range(2):

        @pl.when(where[3] == core)
        def _():
            place(pieces[0:4], pieces[8:12], core)
            place(pieces[4:8], pieces[12:16], 1 - core)

    if has_gain:
        a, b, c, d = (piece[2 * step :, :].astype(F32) for piece in pieces[8:12])
        total = (a + b) + (c + d)
        k = D // w
        both = total[:k] + total[k : 2 * k]
        for j in range(k):
            outs[2][:, j * w : (j + 1) * w] = both[j : j + 1, :]


def events_kernel(events, gain, top, bottom, top_x, bottom_x, grad):
    half = events.shape[0] // 2
    for i, (mine, other) in enumerate(((top, top_x), (bottom, bottom_x))):
        rows = pl.ds(i * half, half)
        x = events[rows, :].astype(F32)
        inverse = lax.rsqrt(jnp.mean(x * x, axis=1, keepdims=True) + 1e-06)
        gn = mine[...].astype(F32) + other[...].astype(F32)
        scaled = gn * gain[...]
        mean = jnp.mean(scaled * x, axis=1, keepdims=True)
        grad[rows, :] = inverse * scaled - x * (inverse * inverse * inverse) * mean


def output_kernel(where, mine, rep, mine_x, rep_x, ow, ow_x, out):
    w = mine.shape[1]
    r = where[3]
    first = pl.ds(pl.multiple_of(r * w, w), w)
    second = pl.ds(pl.multiple_of((1 - r) * w, w), w)
    here = dot_nn(mine[...], ow[first, :]) + dot_nn(rep[...], ow[second, :])
    there = dot_nn(mine_x[...], ow_x[first, :]) + dot_nn(rep_x[...], ow_x[second, :])
    out[...] = (here + there).astype(BF16)


def swap(x, axis, bit=1):
    n = lax.axis_size(axis)
    return lax.ppermute(x, axis, [(i, i ^ bit) for i in range(n)])


def route_even(n):
    return [(2 * i + r, 2 * (i ^ 1) + r) for i in range(n) for r in range(2)]


def route_odd(n):
    route = []
    for i in range(n):
        for r in range(2):
            if i in (0, n - 1):
                route.append((2 * i + r, 2 * i + 1 - r))
            else:
                route.append((2 * i + r, 2 * (((i - 1) ^ 1) + 1) + r))
    return route


def scatter_over_seq(packed):
    me = lax.axis_index("seq")

    def chunk(d):
        return lax.dynamic_index_in_dim(packed, me ^ d, 0, keepdims=False)

    return [chunk(0)] + [swap(chunk(d), "seq", d) for d in (1, 2, 3)]


def gather_over_seq(total):
    return [total] + [swap(total, "seq", d) for d in (1, 2, 3)]


def after(values, *others):
    return lax.optimization_barrier((values, others))[0]


def body(events, norm_gain, in_weight, out_weight, pair_mask, cotangent):
    n_seq, n_head = lax.axis_size("seq"), lax.axis_size("head")
    direct = n_seq == CHUNKS and n_head == 2
    rep, seq = lax.axis_index("rep"), lax.axis_index("seq")
    w = in_weight.shape[2] // 2
    rows2 = 2 * BLOCK
    step = D // CHUNKS
    flip = 1 - seq % 2
    edge = ((seq == 0) | (seq == n_seq - 1)).astype(jnp.int32)
    chunk_ids = [(seq ^ d) if direct else jnp.int32(d) for d in range(CHUNKS)]
    where = jnp.stack([rep ^ flip, flip, edge, rep] + chunk_ids).astype(jnp.int32)

    ev_oth = swap(events, "rep")
    cot_oth = swap(cotangent, "rep")
    mask_oth = swap(pair_mask, "rep")
    scalars = [where, pair_mask, mask_oth]
    gain = norm_gain.reshape(1, D)
    w4 = lax.dynamic_slice(in_weight, (0, 0, rep * w), (D, 4, w)).transpose(1, 0, 2)
    axes = ("seq", "rep")
    even, odd = route_even(n_seq), route_odd(n_seq)

    normed, pre_kv, kv = call(
        project_kv_kernel,
        [shape((rows2, D), BF16), shape((rows2, 2 * w), F32), shape((rows2, 2 * w), BF16)],
        [events, ev_oth, w4, gain],
        [where],
        fetched=3,
    )
    kv_even = lax.ppermute(kv, axes, even)
    kv_odd = lax.ppermute(kv, axes, odd)
    pre_gq, qa, gate, gm = call(
        project_gq_kernel,
        [
            shape((rows2, 2 * w), F32),
            shape((rows2 + MASK_ROWS, 2 * w), BF16),
            shape((rows2, w), BF16),
            shape((rows2, w), F32),
        ],
        [cotangent, cot_oth, w4, out_weight, normed],
        scalars,
        fetched=4,
    )
    qa_even = lax.ppermute(qa, axes, even)
    qa_odd = lax.ppermute(qa, axes, odd)
    acc_shape = shape((rows2, 2 * w), F32)
    q_own, k_own = call(own_kernel, [acc_shape] * 2, [qa, kv], scalars, us=12)
    if n_head == 2:
        ow_x = swap(out_weight, "head")
        late = after(where, ow_x, q_own)
    else:
        late = where
    (q_far,) = call(query_kernel, [acc_shape], [qa, kv_even, kv_odd], [late, pair_mask, mask_oth], us=9)
    mix_own, mix_oth, gp_gq, pack_q = call(
        query_finish_kernel,
        [
            shape((BLOCK, w), BF16),
            shape((BLOCK, w), BF16),
            shape((rows2, 2 * w), BF16),
            shape((CHUNKS, 2 * step + D // CHUNKS, w), BF16),
        ],
        [cotangent, cot_oth, gate, gm, pre_gq, normed, q_own, q_far],
        [where],
    )
    mix_rep = swap(mix_oth, "rep")
    if n_head == 2:
        (output,) = call(
            output_kernel,
            [shape((BLOCK, D), BF16)],
            [mix_own, mix_rep, swap(mix_own, "head"), swap(mix_rep, "head"), out_weight, ow_x],
            [where],
        )
    else:
        weight = jnp.where(rep == 0, out_weight, jnp.roll(out_weight, w, axis=0))
        mixed = jnp.concatenate([mix_own, mix_rep], axis=1)
        output = lax.psum(dot_nn(mixed, weight), "head").astype(BF16)

    (k_far,) = call(functools.partial(key_kernel, KEY_PAIRS[:4]), [acc_shape], [kv, qa_even, qa_odd], [where], us=6)
    if direct:
        got_q = scatter_over_seq(pack_q)
        late = after(where, k_far, got_q)
        (sum_q,) = call(add_chunks_kernel, [shape(got_q[0].shape, BF16)], got_q)
        all_q = gather_over_seq(sum_q)
    else:
        late = where
        sums = lax.psum(pack_q.astype(F32), "seq").astype(BF16)
        all_q = [sums[i] for i in range(CHUNKS)]
    (k_last,) = call(last_key_kernel, [acc_shape], [kv, qa_even, qa_odd, qa], [late, pair_mask, mask_oth], us=6)
    last = after(where, k_last, output, all_q)
    oth_q = [swap(piece, "rep") for piece in all_q]

    pack_kv, gn_own, gn_oth, pg = call(
        key_finish_kernel,
        [
            shape((CHUNKS, 2 * step, w), BF16),
            shape((BLOCK, D), BF16),
            shape((BLOCK, D), BF16),
            shape((1, D), F32),
        ],
        [events, ev_oth, pre_kv, normed, gp_gq, w4, k_own, k_far, k_last],
        [last],
        us=6,
    )
    halves = [shape((BLOCK // 2, D), BF16)] * 2
    top, bottom, pg = call(
        add_cores_kernel,
        halves + [shape((1, D), F32)],
        [gn_own, swap(gn_oth, "rep"), pg, swap(pg, "rep")],
    )
    if direct:
        got_kv = scatter_over_seq(pack_kv)
        top_x, pg_x = swap(top, "head"), swap(pg, "head")
        got_kv = after(got_kv, top_x)
        (sum_kv,) = call(
            add_chunks_gain_kernel, [shape((2 * step + GAIN_ROWS, w), BF16)], got_kv + [pg, pg_x]
        )
        bottom_x = swap(bottom, "head")
        all_kv = gather_over_seq(sum_kv)
    else:
        sums = lax.psum(pack_kv.astype(F32), "seq").astype(BF16)
        all_kv = [sums[i] for i in range(CHUNKS)]
        top, bottom = lax.psum((top.astype(F32), bottom.astype(F32)), "head")
        top_x, bottom_x = jnp.zeros_like(top), jnp.zeros_like(bottom)
    (grad_events,) = call(
        events_kernel, [shape((BLOCK, D), F32)], [events, gain, top, bottom, top_x, bottom_x]
    )
    oth_kv = [swap(piece, "rep") for piece in all_kv]
    outs = call(
        functools.partial(assemble_kernel, direct),
        [shape((D, 4, 2 * w), F32), shape((2 * w, D), F32)] + [shape((1, D), F32)] * direct,
        [*all_q, *oth_q, *all_kv, *oth_kv],
        [where],
    )
    pg = outs[2] if direct else lax.psum(pg, ("seq", "head"))
    return (output, grad_events, outs[0], outs[1], pg.reshape(D))


def solution(mesh):
    return jax.shard_map(
        body,
        mesh=mesh,
        in_specs=(
            P(("grp", "seq", "rep"), None),
            P(),
            P(None, None, "head"),
            P("head", None),
            P(("grp", "seq", "rep"), None),
            P(("grp", "seq", "rep"), None),
        ),
        out_specs=(
            P(("grp", "seq", "rep"), None),
            P(("grp", "seq", "rep"), None),
            P("grp", None, "head"),
            P(("grp", "head"), None),
            P("grp"),
        ),
        check_vma=False,
    )
```

```python
import functools

import jax
import jax.numpy as jnp
from jax import lax
from jax.experimental import pallas as pl
from jax.experimental.pallas import tpu as pltpu
from jax.sharding import PartitionSpec as P

D = 512
E = 64
BLOCK = 512
CHUNKS = 4
MASK_ROWS = 16
GAIN_ROWS = 16
F32 = jnp.float32
BF16 = jnp.bfloat16
VMEM_BYTES = 16 * 1024 * 1024


def dot_nt(a, b):
    return lax.dot_general(a, b, (((1,), (1,)), ((), ())), preferred_element_type=F32)


def dot_tn(a, b):
    return lax.dot_general(a, b, (((0,), (0,)), ((), ())), preferred_element_type=F32)


def dot_nn(a, b):
    return lax.dot_general(a, b, (((1,), (0,)), ((), ())), preferred_element_type=F32)


def sigmoid(x):
    return 0.5 * jnp.tanh(0.5 * x) + 0.5


def silu_slope(x):
    s = sigmoid(x)
    return s * (1.0 + x * (1.0 - s))


def whole(shape):
    zeros = (0,) * len(shape)
    return pl.BlockSpec(shape, lambda *_: zeros)


def call(kernel, out_shapes, args, scalars=(), us=0.0, fetched=0):
    n_scalars, n_out = len(scalars), len(out_shapes)

    def with_fetch(*refs):
        head, held, rest = refs[:n_scalars], refs[n_scalars : n_scalars + fetched], refs[n_scalars + fetched :]
        n_rest = len(args) - fetched + n_out
        slots, sems = rest[n_rest : n_rest + fetched], rest[n_rest + fetched]
        copies = [pltpu.make_async_copy(h, slot, sems.at[i]) for i, (h, slot) in enumerate(zip(held, slots))]
        for copy in copies:
            copy.start()

        def fetch(*which):
            for i in which:
                copies[i].wait()

        kernel(*head, *slots, *rest[:n_rest], fetch)

    scratch = [pltpu.VMEM(a.shape, a.dtype) for a in args[:fetched]]
    return pl.pallas_call(
        with_fetch if fetched else kernel,
        out_shape=out_shapes,
        in_specs=[pl.BlockSpec(memory_space=pltpu.SMEM)] * n_scalars
        + [pl.BlockSpec(memory_space=pltpu.HBM)] * fetched
        + [pl.BlockSpec(memory_space=pltpu.VMEM)] * (len(args) - fetched),
        out_specs=[pl.BlockSpec(memory_space=pltpu.VMEM)] * n_out,
        scratch_shapes=scratch + [pltpu.SemaphoreType.DMA((fetched,))] if fetched else [],
        compiler_params=pltpu.CompilerParams(vmem_limit_bytes=VMEM_BYTES),
        cost_estimate=pl.CostEstimate(flops=int(us * 1.1e9), bytes_accessed=0, transcendentals=0),
    )(*scalars, *args)


def shape(dims, dtype):
    return jax.ShapeDtypeStruct(dims, dtype)


def mask_at(where, mask_own, mask_oth, slot, col):
    at = jnp.where(where[1] == 1, col, 3 - col)
    return jnp.where(where[0] == slot, mask_own[0, at], mask_oth[0, at])


def slots(where):
    mine = where[0]
    return [pl.ds(pl.multiple_of(slot * BLOCK, BLOCK), BLOCK) for slot in (mine, 1 - mine)]


def project_kv_kernel(where, ev_own, ev_oth, w4, gain, normed, pre, kv, fetch):
    fetch(0, 2)
    w_kv = jnp.concatenate([w4[2], w4[3]], axis=1)
    for i, (rows, events) in enumerate(zip(slots(where), (ev_own, ev_oth))):
        if i == 1:
            fetch(1)
        x = events[...].astype(F32)
        inverse = lax.rsqrt(jnp.mean(x * x, axis=1, keepdims=True) + 1e-06)
        n = (x * inverse * gain[...]).astype(BF16)
        normed[rows, :] = n
        p = dot_nn(n, w_kv)
        pre[rows, :] = p
        kv[rows, :] = (p * sigmoid(p)).astype(BF16)


def project_gq_kernel(where, mask_own, mask_oth, cot_own, cot_oth, w4, ow, normed, pre, qa, gate, gm, fetch):
    w = w4.shape[2]
    fetch(0, 2, 3)
    w_gq = jnp.concatenate([w4[0], w4[1]], axis=1)
    wow = ow[pl.ds(pl.multiple_of(where[3] * w, w), w), :]
    for i, (rows, cot) in enumerate(zip(slots(where), (cot_own, cot_oth))):
        if i == 1:
            fetch(1)
        p = dot_nn(normed[rows, :], w_gq)
        pre[rows, :] = p
        act = (p * sigmoid(p)).astype(BF16)
        g = act[:, :w]
        gate[rows, :] = g
        grad_mixed = dot_nt(cot[...], wow)
        gm[rows, :] = grad_mixed
        qa[rows, :w] = act[:, w:]
        qa[rows, w:] = (grad_mixed * g.astype(F32)).astype(BF16)
    lane = lax.broadcasted_iota(jnp.int32, (MASK_ROWS, 2 * w), 1)
    marks = jnp.zeros((MASK_ROWS, 2 * w), F32)
    for slot in range(2):
        for col in range(4):
            m = mask_at(where, mask_own, mask_oth, slot, col).astype(F32)
            marks = jnp.where(lane == 4 * slot + col, m, marks)
    qa[2 * BLOCK :, :] = marks.astype(BF16)


TILE = 256


def pair_side(left, p_slot, right, r_slot, acc):
    w = left.shape[1] // 2
    r_rows = pl.ds(r_slot * BLOCK, BLOCK)
    xr, yr = right[r_rows, :w], right[r_rows, w:]
    lane = lax.broadcasted_iota(jnp.int32, (1, w), 1) // E
    zero = jnp.zeros_like(xr)
    heads = []
    for h in range(w // E):
        on = lane == h
        heads.append((jnp.where(on, xr, zero), jnp.where(on, yr, zero)))
    for t in range(BLOCK // TILE):
        rows = pl.ds(p_slot * BLOCK + t * TILE, TILE)
        x = left[rows, :w] * jnp.asarray(0.5, BF16)
        y = left[rows, w:]
        acc_x = acc[rows, :w]
        acc_y = acc[rows, w:]
        for xh, yh in heads:
            u = dot_nt(x, xh)
            g = dot_nt(y, yh)
            a = 1.0 + jnp.tanh(u)
            m = u * a
            slope = a + m * (2.0 - a)
            acc_y = acc_y + dot_nn(m.astype(BF16), yh)
            acc_x = acc_x + dot_nn((g * slope).astype(BF16), xh)
        acc[rows, :w] = acc_x
        acc[rows, w:] = acc_y


def pair_both(qa, q_slot, kv, k_slot, acc_q, acc_k):
    w = qa.shape[1] // 2
    k_rows = pl.ds(k_slot * BLOCK, BLOCK)
    k, v = kv[k_rows, :w], kv[k_rows, w:]
    lane = lax.broadcasted_iota(jnp.int32, (1, w), 1) // E
    zero = jnp.zeros_like(k)
    grad_k, grad_v = acc_k[k_rows, :w], acc_k[k_rows, w:]
    for t in range(BLOCK // TILE):
        rows = pl.ds(q_slot * BLOCK + t * TILE, TILE)
        q = qa[rows, :w] * jnp.asarray(0.5, BF16)
        ga = qa[rows, w:]
        acc_x = acc_q[rows, :w]
        acc_y = acc_q[rows, w:]
        for h in range(w // E):
            on = lane == h
            kh, vh = jnp.where(on, k, zero), jnp.where(on, v, zero)
            u = dot_nt(q, kh)
            a = 1.0 + jnp.tanh(u)
            m = u * a
            slope = a + m * (2.0 - a)
            weights = m.astype(BF16)
            grad_s = (dot_nt(ga, vh) * slope).astype(BF16)
            acc_y = acc_y + dot_nn(weights, vh)
            acc_x = acc_x + dot_nn(grad_s, kh)
            grad_k = grad_k + 2.0 * dot_tn(grad_s, jnp.where(on, q, jnp.zeros_like(q)))
            grad_v = grad_v + dot_tn(weights, jnp.where(on, ga, jnp.zeros_like(ga)))
        acc_q[rows, :w] = acc_x
        acc_q[rows, w:] = acc_y
    acc_k[k_rows, :w] = grad_k
    acc_k[k_rows, w:] = grad_v


OWN_PAIRS = ((0, 0, None), (1, 1, None), (0, 1, 1), (1, 0, 2))
EVEN_PAIRS = ((0, 0, 2), (1, 0, 3), (0, 1, 3))
ODD_PAIRS = ((1, 1, 1), (0, 1, 0), (1, 0, 0))


def query_kernel(where, mask_own, mask_oth, qa, kv_even, kv_odd, acc):
    acc[...] = jnp.zeros_like(acc)
    for kv, pairs in ((kv_even, EVEN_PAIRS), (kv_odd, ODD_PAIRS)):
        for q_slot, k_slot, col in pairs:
            run = functools.partial(pair_side, qa, q_slot, kv, k_slot, acc)
            pl.when(mask_at(where, mask_own, mask_oth, q_slot, col) == 1)(run)


KEY_PAIRS = tuple((0, *pair) for pair in EVEN_PAIRS) + tuple((1, *pair) for pair in ODD_PAIRS)


def key_kernel(pairs, where, kv, qa_even, qa_odd, acc):
    acc[...] = jnp.zeros_like(acc)
    for odd, q_slot, k_slot, col in pairs:
        qa = qa_odd if odd else qa_even
        marks = qa[2 * BLOCK :, :].astype(F32)
        row = lax.broadcasted_iota(jnp.int32, marks.shape, 0)
        lane = lax.broadcasted_iota(jnp.int32, marks.shape, 1)
        m = jnp.sum(jnp.where((row == 0) & (lane == 4 * q_slot + col), marks, 0.0))
        on = m > 0.5
        if odd:
            on = on & (where[2] == 0)
        pl.when(on)(functools.partial(pair_side, kv, k_slot, qa, q_slot, acc))


def own_kernel(where, mask_own, mask_oth, qa, kv, normed, acc_q, acc_k, normed_t):
    normed_t[...] = normed[...].T
    acc_q[...] = jnp.zeros_like(acc_q)
    acc_k[...] = jnp.zeros_like(acc_k)
    for q_slot, k_slot, col in OWN_PAIRS:
        run = functools.partial(pair_both, qa, q_slot, kv, k_slot, acc_q, acc_k)
        if col is None:
            run()
        else:
            pl.when(mask_at(where, mask_own, mask_oth, q_slot, col) == 1)(run)


def query_finish_kernel(where, cot_own, cot_oth, gate, gm, pre, normed_t, acc_a, acc_b, mix_own, mix_oth, gp, packed):
    w = gate.shape[1]
    grad_out = jnp.zeros((w, D), F32)
    for rows, cot, mixed in zip(slots(where), (cot_own, cot_oth), (mix_own, mix_oth)):
        total = acc_a[rows, :] + acc_b[rows, :]
        grad_query = total[:, :w] * (1.0 / 1024)
        attended = total[:, w:] * (1.0 / 512)
        mix = (attended * gate[rows, :].astype(F32)).astype(BF16)
        mixed[...] = mix
        slope = silu_slope(pre[rows, :])
        gp[rows, :w] = (gm[rows, :] * attended * slope[:, :w]).astype(BF16)
        gp[rows, w:] = (grad_query * slope[:, w:]).astype(BF16)
        grad_out = grad_out + dot_tn(mix, cot[...])
    pack(packed, dot_nn(normed_t[...], gp[...]), grad_out)


def pack(packed, grad_in, grad_out=None):
    step = D // CHUNKS
    w = grad_in.shape[1] // 2
    for c in range(CHUNKS):
        for p in range(2):
            packed[c, p * step : (p + 1) * step, :] = grad_in[c * step : (c + 1) * step, p * w : (p + 1) * w].astype(BF16)
        if grad_out is not None:
            n = w // CHUNKS
            part = grad_out[c * n : (c + 1) * n].astype(BF16)
            for j in range(D // w):
                packed[c, 2 * step + j * n : 2 * step + (j + 1) * n, :] = part[:, j * w : (j + 1) * w]


def key_finish_kernel(
    where, ev_own, ev_oth, pre, normed_t, gp_gq, w4, acc_a, acc_b, acc_c, packed, gn_own, gn_oth, gp
):
    w = pre.shape[1] // 2
    w_gq = jnp.concatenate([w4[0], w4[1]], axis=1)
    w_kv = jnp.concatenate([w4[2], w4[3]], axis=1)
    gain = jnp.zeros((1, D), F32)
    for rows, events, out in zip(slots(where), (ev_own, ev_oth), (gn_own, gn_oth)):
        total = acc_a[rows, :] + acc_b[rows, :] + acc_c[rows, :]
        slope = silu_slope(pre[rows, :])
        gp[rows, :w] = (total[:, :w] * (1.0 / 1024) * slope[:, :w]).astype(BF16)
        gp[rows, w:] = (total[:, w:] * (1.0 / 512) * slope[:, w:]).astype(BF16)
        gn = dot_nt(gp_gq[rows, :], w_gq) + dot_nt(gp[rows, :], w_kv)
        out[...] = gn.astype(BF16)
        x = events[...].astype(F32)
        inverse = lax.rsqrt(jnp.mean(x * x, axis=1, keepdims=True) + 1e-06)
        gain = gain + jnp.sum(gn * x * inverse, axis=0, keepdims=True)
    pack(packed, dot_nn(normed_t[...], gp[...]))
    high = gain.astype(BF16).astype(F32)
    parts = [v[:, j * w : (j + 1) * w] for v in (high, gain - high) for j in range(D // w)]
    if len(parts) < GAIN_ROWS:
        parts.append(jnp.zeros((GAIN_ROWS - len(parts), w), F32))
    for c in range(CHUNKS):
        packed[c, D // CHUNKS * 2 :, :] = jnp.concatenate(parts, axis=0).astype(BF16)


def add_cores_kernel(order, a, b, top, bottom):
    half = BLOCK // 2
    total = (a[...].astype(F32) + b[...].astype(F32)).astype(BF16)
    top[...] = total[:half]
    bottom[...] = total[half:]


def add_chunks_gain_kernel(order, *refs):
    pieces, (bottom, out, wide) = refs[:4], refs[4:]
    n, w = out.shape
    a, b, c, d = (piece[...].astype(F32) for piece in pieces)
    total = (a + b) + (c + d)
    out[...] = total[:n].astype(BF16)
    k = D // w
    rows = [total[n + j : n + j + 1] + total[n + k + j : n + k + j + 1] for j in range(k)]
    gain = jnp.concatenate(rows, axis=1)
    wide[: BLOCK // 2, :] = bottom[...]
    wide[BLOCK // 2 :, :] = split_rows(gain)


def split_rows(total):
    high = total.astype(BF16).astype(F32)
    rest = jnp.zeros((GAIN_ROWS - 2, total.shape[1]), F32)
    return jnp.concatenate([high, total - high, rest], axis=0).astype(BF16)


def join_rows(rows):
    both = rows.astype(F32)
    return both[0:1] + both[1:2]


def add_chunks_kernel(order, a, b, c, d, out):
    out[...] = ((a[...].astype(F32) + b[...].astype(F32)) + (c[...].astype(F32) + d[...].astype(F32))).astype(BF16)


def assemble_kernel(first, where, *refs):
    pieces, rest = refs[:8], refs[8:]
    if first:
        pg_a, pg_b, _, grad_in, pg, parts, sem = rest
        pg[...] = pg_a[...] + pg_b[...]
    else:
        grad_in, grad_out, parts, sem = rest
    w = pieces[0].shape[1]
    step = D // CHUNKS
    n = w // CHUNKS

    def place(i, piece, core):
        lanes = slice(core * w, (core + 1) * w)
        rows = pl.ds(pl.multiple_of(where[4 + i] * step, step), step)
        for p in range(2):
            parts[p, rows, lanes] = piece[p * step : (p + 1) * step, :].astype(F32)
        if first == 0:
            for j in range(D // w):
                block = piece[2 * step + j * n : 2 * step + (j + 1) * n, :]
                out_rows = pl.ds(pl.multiple_of(core * w + where[4 + i] * n, n), n)
                grad_out[out_rows, j * w : (j + 1) * w] = block.astype(F32)

    def copy(i, p):
        rows = pl.ds(pl.multiple_of(where[4 + i] * step, step), step)
        return pltpu.make_async_copy(parts.at[p, rows], grad_in.at[rows, first + p], sem.at[i, p])

    for i in range(CHUNKS):
        for core in range(2):

            @pl.when(where[3] == core)
            def _():
                place(i, pieces[i], core)
                place(i, pieces[4 + i], 1 - core)

        for p in range(2):
            copy(i, p).start()
    for i in range(CHUNKS):
        for p in range(2):
            copy(i, p).wait()


def events_kernel(events, gain, top, bottom, top_x, bottom_x, grad, pg):
    half = BLOCK // 2
    for i, (mine, other) in enumerate(((top, top_x), (bottom, bottom_x))):
        rows = pl.ds(i * half, half)
        x = events[rows, :].astype(F32)
        inverse = lax.rsqrt(jnp.mean(x * x, axis=1, keepdims=True) + 1e-06)
        gn = mine[:half, :].astype(F32) + other[:half, :].astype(F32)
        scaled = gn * gain[...]
        mean = jnp.mean(scaled * x, axis=1, keepdims=True)
        grad[rows, :] = inverse * scaled - x * (inverse * inverse * inverse) * mean
    pg[...] = join_rows(bottom[half:, :]) + join_rows(bottom_x[half:, :])


def output_kernel(where, mine, rep, mine_x, rep_x, ow, ow_x, out):
    w = mine.shape[1]
    r = where[3]
    first = pl.ds(pl.multiple_of(r * w, w), w)
    second = pl.ds(pl.multiple_of((1 - r) * w, w), w)
    here = dot_nn(mine[...], ow[first, :]) + dot_nn(rep[...], ow[second, :])
    there = dot_nn(mine_x[...], ow_x[first, :]) + dot_nn(rep_x[...], ow_x[second, :])
    out[...] = (here + there).astype(BF16)


def swap(x, axis, bit=1):
    n = lax.axis_size(axis)
    return lax.ppermute(x, axis, [(i, i ^ bit) for i in range(n)])


def route_even(n):
    return [(2 * i + r, 2 * (i ^ 1) + r) for i in range(n) for r in range(2)]


def route_odd(n):
    route = []
    for i in range(n):
        for r in range(2):
            if i in (0, n - 1):
                route.append((2 * i + r, 2 * i + 1 - r))
            else:
                route.append((2 * i + r, 2 * (((i - 1) ^ 1) + 1) + r))
    return route


def scatter_over_seq(packed):
    me = lax.axis_index("seq")

    def chunk(d):
        return lax.dynamic_index_in_dim(packed, me ^ d, 0, keepdims=False)

    return [chunk(0)] + [swap(chunk(d), "seq", d) for d in (1, 2, 3)]


def gather_over_seq(total):
    return [total] + [swap(total, "seq", d) for d in (1, 2, 3)]


def after(values, *others):
    return lax.optimization_barrier((values, others))[0]


def body(events, norm_gain, in_weight, out_weight, pair_mask, cotangent):
    n_seq, n_head = lax.axis_size("seq"), lax.axis_size("head")
    direct = n_seq == CHUNKS and n_head == 2
    rep, seq = lax.axis_index("rep"), lax.axis_index("seq")
    w = in_weight.shape[2] // 2
    rows2 = 2 * BLOCK
    step = D // CHUNKS
    flip = 1 - seq % 2
    edge = ((seq == 0) | (seq == n_seq - 1)).astype(jnp.int32)
    chunk_ids = [(seq ^ d) if direct else jnp.int32(d) for d in range(CHUNKS)]
    where = jnp.stack([rep ^ flip, flip, edge, rep] + chunk_ids).astype(jnp.int32)

    ev_oth = swap(events, "rep")
    cot_oth = swap(cotangent, "rep")
    mask_oth = swap(pair_mask, "rep")
    scalars = [where, pair_mask, mask_oth]
    gain = norm_gain.reshape(1, D)
    w4 = lax.dynamic_slice(in_weight, (0, 0, rep * w), (D, 4, w)).transpose(1, 0, 2)
    axes = ("seq", "rep")
    even, odd = route_even(n_seq), route_odd(n_seq)

    normed, pre_kv, kv = call(
        project_kv_kernel,
        [shape((rows2, D), BF16), shape((rows2, 2 * w), F32), shape((rows2, 2 * w), BF16)],
        [events, ev_oth, w4, gain],
        [where],
        fetched=3,
    )
    kv_even = lax.ppermute(kv, axes, even)
    kv_odd = lax.ppermute(kv, axes, odd)
    pre_gq, qa, gate, gm = call(
        project_gq_kernel,
        [
            shape((rows2, 2 * w), F32),
            shape((rows2 + MASK_ROWS, 2 * w), BF16),
            shape((rows2, w), BF16),
            shape((rows2, w), F32),
        ],
        [cotangent, cot_oth, w4, out_weight, normed],
        scalars,
        fetched=4,
    )
    qa_even = lax.ppermute(qa, axes, even)
    qa_odd = lax.ppermute(qa, axes, odd)
    acc_shape = shape((rows2, 2 * w), F32)
    q_own, k_own, normed_t = call(
        own_kernel, [acc_shape, acc_shape, shape((D, rows2), BF16)], [qa, kv, normed], scalars, us=9
    )
    late = where
    if n_head == 2:
        ow_x = swap(out_weight, "head")
        late = after(where, ow_x, q_own)
    (q_far,) = call(query_kernel, [acc_shape], [qa, kv_even, kv_odd], [late, pair_mask, mask_oth], us=9)
    mix_own, mix_oth, gp_gq, pack_q = call(
        query_finish_kernel,
        [
            shape((BLOCK, w), BF16),
            shape((BLOCK, w), BF16),
            shape((rows2, 2 * w), BF16),
            shape((CHUNKS, 2 * step + D // CHUNKS, w), BF16),
        ],
        [cotangent, cot_oth, gate, gm, pre_gq, normed_t, q_own, q_far],
        [where],
    )
    mix_rep = swap(mix_oth, "rep")
    (k_far,) = call(functools.partial(key_kernel, KEY_PAIRS[:3]), [acc_shape], [kv, qa_even, qa_odd], [where], us=6)
    add_shape = shape((2 * step + D // CHUNKS, w), BF16)
    if direct:
        mixed_x = [swap(mix_own, "head"), swap(mix_rep, "head")]
        got_q = scatter_over_seq(pack_q)
        late = after(where, k_far, got_q)
        (sum_q,) = call(add_chunks_kernel, [add_shape], got_q, [where])
        all_q = gather_over_seq(sum_q)
    else:
        mixed_x = []
        late = where
        sums = lax.psum(pack_q.astype(F32), "seq").astype(BF16)
        all_q = [sums[i] for i in range(CHUNKS)]
    (k_last,) = call(functools.partial(key_kernel, KEY_PAIRS[3:]), [acc_shape], [kv, qa_even, qa_odd], [late], us=6)
    oth_q = [swap(piece, "rep") for piece in all_q]
    last = after(where, k_last, mixed_x, all_q)

    pack_kv, gn_own, gn_oth, _ = call(
        key_finish_kernel,
        [
            shape((CHUNKS, 2 * step + GAIN_ROWS, w), BF16),
            shape((BLOCK, D), BF16),
            shape((BLOCK, D), BF16),
            shape((rows2, 2 * w), BF16),
        ],
        [events, ev_oth, pre_kv, normed_t, gp_gq, w4, k_own, k_far, k_last],
        [last],
    )
    late = where
    if direct:
        got_kv = scatter_over_seq(pack_kv)
        late = after(where, got_kv[1])
    halves = [shape((BLOCK // 2, D), BF16)] * 2
    top, bottom = call(add_cores_kernel, halves, [gn_own, swap(gn_oth, "rep")], [late])
    if n_head == 2:
        (output,) = call(
            output_kernel,
            [shape((BLOCK, D), BF16)],
            [mix_own, mix_rep, *(mixed_x or [swap(mix_own, "head"), swap(mix_rep, "head")]), out_weight, ow_x],
            [where],
        )
        top_x = swap(top, "head")
    else:
        weight = jnp.where(rep == 0, out_weight, jnp.roll(out_weight, w, axis=0))
        mixed = jnp.concatenate([mix_own, mix_rep], axis=1)
        output = lax.psum(dot_nn(mixed, weight), "head").astype(BF16)
        top, bottom = lax.psum((top.astype(F32), bottom.astype(F32)), "head")
        top_x = jnp.zeros_like(top)
    wide = shape((BLOCK // 2 + GAIN_ROWS, D), BF16)
    if direct:
        sum_kv, bottom = call(
            add_chunks_gain_kernel,
            [shape((2 * step, w), BF16), wide],
            [*got_kv, bottom],
            [after(where, output)],
        )
        bottom_x = swap(bottom, "head")
        all_kv = gather_over_seq(sum_kv)
        late = after(where, all_kv[1])
    else:
        sums = lax.psum(pack_kv.astype(F32), "seq")
        all_kv = [sums[i, : 2 * step].astype(BF16) for i in range(CHUNKS)]
        pg = sums[0, 2 * step :]
        pg = (pg[: D // w] + pg[D // w : 2 * (D // w)]).reshape(1, D)
        pg = jnp.concatenate([pg, jnp.zeros((GAIN_ROWS - 1, D), F32)])
        bottom, bottom_x = jnp.concatenate([bottom, lax.psum(pg, "head")]), jnp.zeros(wide.shape, F32)
    grad_events, pg = call(
        events_kernel,
        [shape((BLOCK, D), F32), shape((1, D), F32)],
        [events, gain, top, bottom, top_x, bottom_x],
    )
    grad_in, grad_out = assemble(late, [*all_q, *oth_q], w)
    all_kv = after(all_kv, grad_out)
    oth_kv = [swap(piece, "rep") for piece in all_kv]
    grad_in, pg = assemble(where, [*all_kv, *oth_kv, pg, swap(pg, "rep")], w, grad_in)
    return (output, grad_events, grad_in, grad_out, pg.reshape(D))


def assemble(where, pieces, w, grad_in=None):
    held = [] if grad_in is None else [grad_in]
    hbm, vmem = pl.BlockSpec(memory_space=pltpu.HBM), pl.BlockSpec(memory_space=pltpu.VMEM)
    return pl.pallas_call(
        functools.partial(assemble_kernel, 2 * len(held)),
        out_shape=[shape((D, 4, 2 * w), F32), shape((1, D) if held else (2 * w, D), F32)],
        in_specs=[pl.BlockSpec(memory_space=pltpu.SMEM)] + [vmem] * len(pieces) + [hbm] * len(held),
        out_specs=[hbm, vmem],
        input_output_aliases={1 + len(pieces): 0} if held else {},
        scratch_shapes=[pltpu.VMEM((2, D, 2 * w), F32), pltpu.SemaphoreType.DMA((CHUNKS, 2))],
        compiler_params=pltpu.CompilerParams(vmem_limit_bytes=VMEM_BYTES),
        cost_estimate=pl.CostEstimate(flops=0, bytes_accessed=0, transcendentals=0),
    )(where, *pieces, *held)


def solution(mesh):
    return jax.shard_map(
        body,
        mesh=mesh,
        in_specs=(
            P(("grp", "seq", "rep"), None),
            P(),
            P(None, None, "head"),
            P("head", None),
            P(("grp", "seq", "rep"), None),
            P(("grp", "seq", "rep"), None),
        ),
        out_specs=(
            P(("grp", "seq", "rep"), None),
            P(("grp", "seq", "rep"), None),
            P("grp", None, "head"),
            P(("grp", "head"), None),
            P("grp"),
        ),
        check_vma=False,
    )
```

```python
import functools

import jax
import jax.numpy as jnp
from jax import lax
from jax.experimental import pallas as pl
from jax.experimental.pallas import tpu as pltpu
from jax.sharding import PartitionSpec as P

D = 512
E = 64
BLOCK = 512
CHUNKS = 4
MASK_ROWS = 16
GAIN_ROWS = 16
TOP = 320
LANES = 128
F32 = jnp.float32
BF16 = jnp.bfloat16
VMEM_BYTES = 16 * 1024 * 1024


def dot_nt(a, b):
    return lax.dot_general(a, b, (((1,), (1,)), ((), ())), preferred_element_type=F32)


def dot_tn(a, b):
    return lax.dot_general(a, b, (((0,), (0,)), ((), ())), preferred_element_type=F32)


def dot_nn(a, b):
    return lax.dot_general(a, b, (((1,), (0,)), ((), ())), preferred_element_type=F32)


def sigmoid(x):
    return 0.5 * jnp.tanh(0.5 * x) + 0.5


def whole(shape):
    zeros = (0,) * len(shape)
    return pl.BlockSpec(shape, lambda *_: zeros)


def call(kernel, out_shapes, args, scalars=(), us=0.0, fetched=0):
    n_scalars, n_out = len(scalars), len(out_shapes)

    def with_fetch(*refs):
        head, held, rest = refs[:n_scalars], refs[n_scalars : n_scalars + fetched], refs[n_scalars + fetched :]
        n_rest = len(args) - fetched + n_out
        slots, sems = rest[n_rest : n_rest + fetched], rest[n_rest + fetched]
        copies = [pltpu.make_async_copy(h, slot, sems.at[i]) for i, (h, slot) in enumerate(zip(held, slots))]
        for copy in copies:
            copy.start()

        def fetch(*which):
            for i in which:
                copies[i].wait()

        kernel(*head, *slots, *rest[:n_rest], fetch)

    scratch = [pltpu.VMEM(a.shape, a.dtype) for a in args[:fetched]]
    return pl.pallas_call(
        with_fetch if fetched else kernel,
        out_shape=out_shapes,
        in_specs=[pl.BlockSpec(memory_space=pltpu.SMEM)] * n_scalars
        + [pl.BlockSpec(memory_space=pltpu.HBM)] * fetched
        + [pl.BlockSpec(memory_space=pltpu.VMEM)] * (len(args) - fetched),
        out_specs=[pl.BlockSpec(memory_space=pltpu.VMEM)] * n_out,
        scratch_shapes=scratch + [pltpu.SemaphoreType.DMA((fetched,))] if fetched else [],
        compiler_params=pltpu.CompilerParams(vmem_limit_bytes=VMEM_BYTES),
        cost_estimate=pl.CostEstimate(flops=int(us * 1.1e9), bytes_accessed=0, transcendentals=0),
    )(*scalars, *args)


def shape(dims, dtype):
    return jax.ShapeDtypeStruct(dims, dtype)


def mask_at(where, mask_own, mask_oth, slot, col):
    at = jnp.where(where[1] == 1, col, 3 - col)
    return jnp.where(where[0] == slot, mask_own[0, at], mask_oth[0, at])


def slots(where):
    mine = where[0]
    return [pl.ds(pl.multiple_of(slot * BLOCK, BLOCK), BLOCK) for slot in (mine, 1 - mine)]


def project_kv_kernel(where, ev_own, ev_oth, w4, gain, normed, inv, slope, kv, fetch):
    fetch(0, 2)
    w_kv = jnp.concatenate([w4[2], w4[3]], axis=1)
    for i, (rows, events) in enumerate(zip(slots(where), (ev_own, ev_oth))):
        if i == 1:
            fetch(1)
        x = events[...].astype(F32)
        inverse = lax.rsqrt(jnp.mean(x * x, axis=1, keepdims=True) + 1e-06)
        n = (x * inverse * gain[...]).astype(BF16)
        normed[rows, :] = n
        inv[rows, :] = jnp.broadcast_to(inverse, (BLOCK, LANES))
        p = dot_nn(n, w_kv)
        s = sigmoid(p)
        slope[rows, :] = s * (1.0 + p * (1.0 - s))
        kv[rows, :] = (p * s).astype(BF16)


def project_gq_kernel(where, mask_own, mask_oth, cot_own, cot_oth, w4, ow, normed, slope, qa, gate, gm, fetch):
    w = w4.shape[2]
    fetch(0, 2, 3)
    w_gq = jnp.concatenate([w4[0], w4[1]], axis=1)
    wow = ow[pl.ds(pl.multiple_of(where[3] * w, w), w), :]
    for i, (rows, cot) in enumerate(zip(slots(where), (cot_own, cot_oth))):
        if i == 1:
            fetch(1)
        p = dot_nn(normed[rows, :], w_gq)
        s = sigmoid(p)
        slope[rows, :] = s * (1.0 + p * (1.0 - s))
        act = (p * s).astype(BF16)
        g = act[:, :w]
        gate[rows, :] = g
        grad_mixed = dot_nt(cot[...], wow)
        gm[rows, :] = grad_mixed
        qa[rows, :w] = act[:, w:]
        qa[rows, w:] = (grad_mixed * g.astype(F32)).astype(BF16)
    lane = lax.broadcasted_iota(jnp.int32, (MASK_ROWS, 2 * w), 1)
    marks = jnp.zeros((MASK_ROWS, 2 * w), F32)
    for slot in range(2):
        for col in range(4):
            m = mask_at(where, mask_own, mask_oth, slot, col).astype(F32)
            marks = jnp.where(lane == 4 * slot + col, m, marks)
    qa[2 * BLOCK :, :] = marks.astype(BF16)


TILE = 512


def pair_side(left, l_slots, right, r_slot, acc):
    w = left.shape[1] // 2
    r_rows = pl.ds(r_slot * BLOCK, BLOCK)
    xr, yr = right[r_rows, :w], right[r_rows, w:]
    lane = lax.broadcasted_iota(jnp.int32, (1, w), 1) // E
    zero = jnp.zeros_like(xr)
    heads = []
    for h in range(w // E):
        on = lane == h
        heads.append((jnp.where(on, xr, zero), jnp.where(on, yr, zero)))
    for slot in l_slots:
        rows = pl.ds(slot * BLOCK, BLOCK)
        x = left[rows, :w] * jnp.asarray(0.5, BF16)
        y = left[rows, w:]
        acc_x = acc[rows, :w]
        acc_y = acc[rows, w:]
        for xh, yh in heads:
            u = dot_nt(x, xh)
            g = dot_nt(y, yh)
            a = 1.0 + jnp.tanh(u)
            m = u * a
            slope = a + m * (2.0 - a)
            acc_y = acc_y + dot_nn(m.astype(BF16), yh)
            acc_x = acc_x + dot_nn((g * slope).astype(BF16), xh)
        acc[rows, :w] = acc_x
        acc[rows, w:] = acc_y


def sides(left, right, acc, pairs):
    (l0, r0, on0), (l1, r1, on1), (l2, r2, on2) = pairs
    pl.when(on0 & on1)(functools.partial(pair_side, left, (l0, l1), right, r0, acc))
    pl.when(on0 & ~on1)(functools.partial(pair_side, left, (l0,), right, r0, acc))
    pl.when(on1 & ~on0)(functools.partial(pair_side, left, (l1,), right, r1, acc))
    pl.when(on2)(functools.partial(pair_side, left, (l2,), right, r2, acc))


def pair_both(qa, q_slot, kv, k_slot, acc_q, acc_k):
    w = qa.shape[1] // 2
    k_rows = pl.ds(k_slot * BLOCK, BLOCK)
    k, v = kv[k_rows, :w], kv[k_rows, w:]
    lane = lax.broadcasted_iota(jnp.int32, (1, w), 1) // E
    zero = jnp.zeros_like(k)
    grad_k, grad_v = acc_k[k_rows, :w], acc_k[k_rows, w:]
    for t in range(BLOCK // TILE):
        rows = pl.ds(q_slot * BLOCK + t * TILE, TILE)
        q = qa[rows, :w] * jnp.asarray(0.5, BF16)
        ga = qa[rows, w:]
        acc_x = acc_q[rows, :w]
        acc_y = acc_q[rows, w:]
        for h in range(w // E):
            on = lane == h
            kh, vh = jnp.where(on, k, zero), jnp.where(on, v, zero)
            u = dot_nt(q, kh)
            a = 1.0 + jnp.tanh(u)
            m = u * a
            slope = a + m * (2.0 - a)
            weights = m.astype(BF16)
            grad_s = (dot_nt(ga, vh) * slope).astype(BF16)
            acc_y = acc_y + dot_nn(weights, vh)
            acc_x = acc_x + dot_nn(grad_s, kh)
            grad_k = grad_k + 2.0 * dot_tn(grad_s, jnp.where(on, q, jnp.zeros_like(q)))
            grad_v = grad_v + dot_tn(weights, jnp.where(on, ga, jnp.zeros_like(ga)))
        acc_q[rows, :w] = acc_x
        acc_q[rows, w:] = acc_y
    acc_k[k_rows, :w] = grad_k
    acc_k[k_rows, w:] = grad_v


OWN_PAIRS = ((0, 0, None), (1, 1, None), (0, 1, 1), (1, 0, 2))
EVEN_PAIRS = ((0, 0, 2), (1, 0, 3), (0, 1, 3))
ODD_PAIRS = ((1, 1, 1), (0, 1, 0), (1, 0, 0))


def query_kernel(pairs, where, mask_own, mask_oth, qa, kv, acc):
    acc[...] = jnp.zeros_like(acc)
    on = [mask_at(where, mask_own, mask_oth, q_slot, col) == 1 for q_slot, _, col in pairs]
    sides(qa, kv, acc, [(q_slot, k_slot, m) for (q_slot, k_slot, _), m in zip(pairs, on)])


def key_kernel(pairs, where, kv, qa, acc):
    acc[...] = jnp.zeros_like(acc)
    marks = qa[2 * BLOCK :, :].astype(F32)
    row = lax.broadcasted_iota(jnp.int32, marks.shape, 0)
    lane = lax.broadcasted_iota(jnp.int32, marks.shape, 1)
    group = []
    for at in (0, 2, 1):
        q_slot, k_slot, col = pairs[at]
        m = jnp.sum(jnp.where((row == 0) & (lane == 4 * q_slot + col), marks, 0.0))
        on = m > 0.5
        if pairs is ODD_PAIRS:
            on = on & (where[2] == 0)
        group.append((k_slot, q_slot, on))
    sides(kv, qa, acc, group)


def own_kernel(where, mask_own, mask_oth, qa, kv, normed, acc_q, acc_k, normed_t):
    normed_t[...] = normed[...].T
    acc_q[...] = jnp.zeros_like(acc_q)
    acc_k[...] = jnp.zeros_like(acc_k)
    for q_slot, k_slot, col in OWN_PAIRS:
        run = functools.partial(pair_both, qa, q_slot, kv, k_slot, acc_q, acc_k)
        if col is None:
            run()
        else:
            pl.when(mask_at(where, mask_own, mask_oth, q_slot, col) == 1)(run)


def query_finish_kernel(where, cot_own, cot_oth, gate, gm, slopes, normed_t, acc_a, acc_b, acc_c, mix_own, mix_oth, gp, packed):
    w = gate.shape[1]
    grad_out = jnp.zeros((w, D), F32)
    for rows, cot, mixed in zip(slots(where), (cot_own, cot_oth), (mix_own, mix_oth)):
        total = acc_a[rows, :] + acc_b[rows, :] + acc_c[rows, :]
        grad_query = total[:, :w] * (1.0 / 1024)
        attended = total[:, w:] * (1.0 / 512)
        mix = (attended * gate[rows, :].astype(F32)).astype(BF16)
        mixed[...] = mix
        slope = slopes[rows, :]
        gp[rows, :w] = (gm[rows, :] * attended * slope[:, :w]).astype(BF16)
        gp[rows, w:] = (grad_query * slope[:, w:]).astype(BF16)
        grad_out = grad_out + dot_tn(mix, cot[...])
    pack(packed, dot_nn(normed_t[...], gp[...]), grad_out)


def pack(packed, grad_in, grad_out=None):
    step = D // CHUNKS
    w = grad_in.shape[1] // 2
    for c in range(CHUNKS):
        for p in range(2):
            packed[c, p * step : (p + 1) * step, :] = grad_in[c * step : (c + 1) * step, p * w : (p + 1) * w].astype(BF16)
        if grad_out is not None:
            n = w // CHUNKS
            part = grad_out[c * n : (c + 1) * n].astype(BF16)
            for j in range(D // w):
                packed[c, 2 * step + j * n : 2 * step + (j + 1) * n, :] = part[:, j * w : (j + 1) * w]


def key_finish_kernel(
    where, ev_own, ev_oth, inv, slopes, normed_t, gp_gq, w4, acc_a, acc_b, acc_c, packed, gn_own, gn_oth, gp
):
    w = slopes.shape[1] // 2
    w_gq = jnp.concatenate([w4[0], w4[1]], axis=1)
    w_kv = jnp.concatenate([w4[2], w4[3]], axis=1)
    gain = jnp.zeros((1, D), F32)
    for rows, events, out in zip(slots(where), (ev_own, ev_oth), (gn_own, gn_oth)):
        total = acc_a[rows, :] + acc_b[rows, :] + acc_c[rows, :]
        slope = slopes[rows, :]
        gp[rows, :w] = (total[:, :w] * (1.0 / 1024) * slope[:, :w]).astype(BF16)
        gp[rows, w:] = (total[:, w:] * (1.0 / 512) * slope[:, w:]).astype(BF16)
        gn = dot_nt(gp_gq[rows, :], w_gq) + dot_nt(gp[rows, :], w_kv)
        out[...] = gn.astype(BF16)
        inverse = jnp.concatenate([inv[rows, :]] * (D // LANES), axis=1)
        gain = gain + jnp.sum(gn * events[...].astype(F32) * inverse, axis=0, keepdims=True)
    pack(packed, dot_nn(normed_t[...], gp[...]))
    high = gain.astype(BF16).astype(F32)
    parts = [v[:, j * w : (j + 1) * w] for v in (high, gain - high) for j in range(D // w)]
    if len(parts) < GAIN_ROWS:
        parts.append(jnp.zeros((GAIN_ROWS - len(parts), w), F32))
    for c in range(CHUNKS):
        packed[c, D // CHUNKS * 2 :, :] = jnp.concatenate(parts, axis=0).astype(BF16)


def add_cores_kernel(order, a, b, top, bottom):
    total = (a[...].astype(F32) + b[...].astype(F32)).astype(BF16)
    top[...] = total[:TOP]
    bottom[...] = total[TOP:]


def add_chunks_gain_kernel(order, *refs):
    pieces, (bottom, out, wide) = refs[:4], refs[4:]
    n, w = out.shape
    a, b, c, d = (piece[...].astype(F32) for piece in pieces)
    total = (a + b) + (c + d)
    out[...] = total[:n].astype(BF16)
    k = D // w
    rows = [total[n + j : n + j + 1] + total[n + k + j : n + k + j + 1] for j in range(k)]
    gain = jnp.concatenate(rows, axis=1)
    wide[: BLOCK - TOP, :] = bottom[...]
    wide[BLOCK - TOP :, :] = split_rows(gain)


def split_rows(total):
    high = total.astype(BF16).astype(F32)
    rest = jnp.zeros((GAIN_ROWS - 2, total.shape[1]), F32)
    return jnp.concatenate([high, total - high, rest], axis=0).astype(BF16)


def join_rows(rows):
    both = rows.astype(F32)
    return both[0:1] + both[1:2]


def add_chunks_kernel(order, a, b, c, d, out):
    out[...] = ((a[...].astype(F32) + b[...].astype(F32)) + (c[...].astype(F32) + d[...].astype(F32))).astype(BF16)


def assemble_kernel(first, where, *refs):
    pieces, rest = refs[:8], refs[8:]
    if first:
        pg_a, pg_b, _, grad_in, pg, parts, sem = rest
        pg[...] = pg_a[...] + pg_b[...]
    else:
        grad_in, grad_out, parts, sem = rest
    w = pieces[0].shape[1]
    step = D // CHUNKS
    n = w // CHUNKS

    def place(i, piece, core):
        lanes = slice(core * w, (core + 1) * w)
        rows = pl.ds(pl.multiple_of(where[4 + i] * step, step), step)
        for p in range(2):
            parts[p, rows, lanes] = piece[p * step : (p + 1) * step, :].astype(F32)
        if first == 0:
            for j in range(D // w):
                block = piece[2 * step + j * n : 2 * step + (j + 1) * n, :]
                out_rows = pl.ds(pl.multiple_of(core * w + where[4 + i] * n, n), n)
                grad_out[out_rows, j * w : (j + 1) * w] = block.astype(F32)

    def copy(i, p):
        rows = pl.ds(pl.multiple_of(where[4 + i] * step, step), step)
        return pltpu.make_async_copy(parts.at[p, rows], grad_in.at[rows, first + p], sem.at[i, p])

    for i in range(CHUNKS):
        for core in range(2):

            @pl.when(where[3] == core)
            def _():
                place(i, pieces[i], core)
                place(i, pieces[4 + i], 1 - core)

        for p in range(2):
            copy(i, p).start()
    for i in range(CHUNKS):
        for p in range(2):
            copy(i, p).wait()


def events_kernel(events, gain, top, bottom, top_x, bottom_x, grad, pg):
    for start, rows, mine, other in ((0, TOP, top, top_x), (TOP, BLOCK - TOP, bottom, bottom_x)):
        x = events[start : start + rows, :].astype(F32)
        inverse = lax.rsqrt(jnp.mean(x * x, axis=1, keepdims=True) + 1e-06)
        gn = mine[:rows, :].astype(F32) + other[:rows, :].astype(F32)
        scaled = gn * gain[...]
        mean = jnp.mean(scaled * x, axis=1, keepdims=True)
        grad[start : start + rows, :] = inverse * scaled - x * (inverse * inverse * inverse) * mean
    pg[...] = join_rows(bottom[BLOCK - TOP :, :]) + join_rows(bottom_x[BLOCK - TOP :, :])


def output_kernel(where, mine, rep, mine_x, rep_x, ow, ow_x, out):
    w = mine.shape[1]
    r = where[3]
    first = pl.ds(pl.multiple_of(r * w, w), w)
    second = pl.ds(pl.multiple_of((1 - r) * w, w), w)
    here = dot_nn(mine[...], ow[first, :]) + dot_nn(rep[...], ow[second, :])
    there = dot_nn(mine_x[...], ow_x[first, :]) + dot_nn(rep_x[...], ow_x[second, :])
    out[...] = (here + there).astype(BF16)


def swap(x, axis, bit=1):
    n = lax.axis_size(axis)
    return lax.ppermute(x, axis, [(i, i ^ bit) for i in range(n)])


def route_even(n):
    return [(2 * i + r, 2 * (i ^ 1) + r) for i in range(n) for r in range(2)]


def route_odd(n):
    route = []
    for i in range(n):
        for r in range(2):
            if i in (0, n - 1):
                route.append((2 * i + r, 2 * i + 1 - r))
            else:
                route.append((2 * i + r, 2 * (((i - 1) ^ 1) + 1) + r))
    return route


def scatter_over_seq(packed):
    me = lax.axis_index("seq")

    def chunk(d):
        return lax.dynamic_index_in_dim(packed, me ^ d, 0, keepdims=False)

    return [chunk(0)] + [swap(chunk(d), "seq", d) for d in (1, 2, 3)]


def gather_over_seq(total):
    return [total] + [swap(total, "seq", d) for d in (1, 2, 3)]


def after(values, *others):
    return lax.optimization_barrier((values, others))[0]


def body(events, norm_gain, in_weight, out_weight, pair_mask, cotangent):
    n_seq, n_head = lax.axis_size("seq"), lax.axis_size("head")
    direct = n_seq == CHUNKS and n_head == 2
    rep, seq = lax.axis_index("rep"), lax.axis_index("seq")
    w = in_weight.shape[2] // 2
    rows2 = 2 * BLOCK
    step = D // CHUNKS
    flip = 1 - seq % 2
    edge = ((seq == 0) | (seq == n_seq - 1)).astype(jnp.int32)
    chunk_ids = [(seq ^ d) if direct else jnp.int32(d) for d in range(CHUNKS)]
    where = jnp.stack([rep ^ flip, flip, edge, rep] + chunk_ids).astype(jnp.int32)

    ev_oth = swap(events, "rep")
    cot_oth = swap(cotangent, "rep")
    mask_oth = swap(pair_mask, "rep")
    scalars = [where, pair_mask, mask_oth]
    gain = norm_gain.reshape(1, D)
    w4 = lax.dynamic_slice(in_weight, (0, 0, rep * w), (D, 4, w)).transpose(1, 0, 2)
    axes = ("seq", "rep")
    even, odd = route_even(n_seq), route_odd(n_seq)

    normed, inv, slope_kv, kv = call(
        project_kv_kernel,
        [shape((rows2, D), BF16), shape((rows2, LANES), F32), shape((rows2, 2 * w), F32), shape((rows2, 2 * w), BF16)],
        [events, ev_oth, w4, gain],
        [where],
        fetched=3,
    )
    kv_even = lax.ppermute(kv, axes, even)
    kv_odd = lax.ppermute(kv, axes, odd)
    slope_gq, qa, gate, gm = call(
        project_gq_kernel,
        [
            shape((rows2, 2 * w), F32),
            shape((rows2 + MASK_ROWS, 2 * w), BF16),
            shape((rows2, w), BF16),
            shape((rows2, w), F32),
        ],
        [cotangent, cot_oth, w4, out_weight, normed],
        scalars,
        fetched=4,
    )
    qa_even = lax.ppermute(qa, axes, even)
    qa_odd = lax.ppermute(qa, axes, odd)
    acc_shape = shape((rows2, 2 * w), F32)
    q_own, k_own, normed_t = call(
        own_kernel, [acc_shape, acc_shape, shape((D, rows2), BF16)], [qa, kv, normed], scalars, us=9
    )
    (q_even,) = call(functools.partial(query_kernel, EVEN_PAIRS), [acc_shape], [qa, kv_even], scalars, us=5)
    late = where
    if n_head == 2:
        ow_x = swap(out_weight, "head")
        late = after(where, ow_x, q_even)
    (q_odd,) = call(
        functools.partial(query_kernel, ODD_PAIRS), [acc_shape], [qa, kv_odd], [late, pair_mask, mask_oth], us=5
    )
    mix_own, mix_oth, gp_gq, pack_q = call(
        query_finish_kernel,
        [
            shape((BLOCK, w), BF16),
            shape((BLOCK, w), BF16),
            shape((rows2, 2 * w), BF16),
            shape((CHUNKS, 2 * step + D // CHUNKS, w), BF16),
        ],
        [cotangent, cot_oth, gate, gm, slope_gq, normed_t, q_own, q_even, q_odd],
        [where],
    )
    mix_rep = swap(mix_oth, "rep")
    (k_far,) = call(functools.partial(key_kernel, EVEN_PAIRS), [acc_shape], [kv, qa_even], [where], us=6)
    add_shape = shape((2 * step + D // CHUNKS, w), BF16)
    if direct:
        mixed_x = [swap(mix_own, "head"), swap(mix_rep, "head")]
        got_q = scatter_over_seq(pack_q)
        late = after(where, k_far, got_q)
        (sum_q,) = call(add_chunks_kernel, [add_shape], got_q, [where])
        all_q = gather_over_seq(sum_q)
    else:
        mixed_x = []
        late = where
        sums = lax.psum(pack_q.astype(F32), "seq").astype(BF16)
        all_q = [sums[i] for i in range(CHUNKS)]
    (k_last,) = call(functools.partial(key_kernel, ODD_PAIRS), [acc_shape], [kv, qa_odd], [late], us=6)
    oth_q = [swap(piece, "rep") for piece in all_q]
    last = after(where, k_last, mixed_x, all_q)

    pack_kv, gn_own, gn_oth, _ = call(
        key_finish_kernel,
        [
            shape((CHUNKS, 2 * step + GAIN_ROWS, w), BF16),
            shape((BLOCK, D), BF16),
            shape((BLOCK, D), BF16),
            shape((rows2, 2 * w), BF16),
        ],
        [events, ev_oth, inv, slope_kv, normed_t, gp_gq, w4, k_own, k_far, k_last],
        [last],
    )
    late = where
    if direct:
        got_kv = scatter_over_seq(pack_kv)
    halves = [shape((TOP, D), BF16), shape((BLOCK - TOP, D), BF16)]
    top, bottom = call(add_cores_kernel, halves, [gn_own, swap(gn_oth, "rep")], [late])
    if n_head == 2:
        (output,) = call(
            output_kernel,
            [shape((BLOCK, D), BF16)],
            [mix_own, mix_rep, *(mixed_x or [swap(mix_own, "head"), swap(mix_rep, "head")]), out_weight, ow_x],
            [where],
        )
        top_x = swap(top, "head")
    else:
        weight = jnp.where(rep == 0, out_weight, jnp.roll(out_weight, w, axis=0))
        mixed = jnp.concatenate([mix_own, mix_rep], axis=1)
        output = lax.psum(dot_nn(mixed, weight), "head").astype(BF16)
        top, bottom = lax.psum((top.astype(F32), bottom.astype(F32)), "head")
        top_x = jnp.zeros_like(top)
    wide = shape((BLOCK - TOP + GAIN_ROWS, D), BF16)
    if direct:
        sum_kv, bottom = call(
            add_chunks_gain_kernel,
            [shape((2 * step, w), BF16), wide],
            [*got_kv, bottom],
            [after(where, output, oth_q)],
        )
        bottom_x = swap(bottom, "head")
        all_kv = gather_over_seq(sum_kv)
    else:
        sums = lax.psum(pack_kv.astype(F32), "seq")
        all_kv = [sums[i, : 2 * step].astype(BF16) for i in range(CHUNKS)]
        pg = sums[0, 2 * step :]
        pg = (pg[: D // w] + pg[D // w : 2 * (D // w)]).reshape(1, D)
        pg = jnp.concatenate([pg, jnp.zeros((GAIN_ROWS - 1, D), F32)])
        bottom, bottom_x = jnp.concatenate([bottom, lax.psum(pg, "head")]), jnp.zeros(wide.shape, F32)
    grad_events, pg = call(
        events_kernel,
        [shape((BLOCK, D), F32), shape((1, D), F32)],
        [events, gain, top, bottom, top_x, bottom_x],
    )
    grad_in, grad_out = assemble(late, [*all_q, *oth_q], w)
    all_kv = after(all_kv, grad_out, pg)
    oth_kv = [swap(piece, "rep") for piece in all_kv]
    grad_in, pg = assemble(where, [*all_kv, *oth_kv, pg, swap(pg, "rep")], w, grad_in)
    return (output, grad_events, grad_in, grad_out, pg.reshape(D))


def assemble(where, pieces, w, grad_in=None):
    held = [] if grad_in is None else [grad_in]
    hbm, vmem = pl.BlockSpec(memory_space=pltpu.HBM), pl.BlockSpec(memory_space=pltpu.VMEM)
    return pl.pallas_call(
        functools.partial(assemble_kernel, 2 * len(held)),
        out_shape=[shape((D, 4, 2 * w), F32), shape((1, D) if held else (2 * w, D), F32)],
        in_specs=[pl.BlockSpec(memory_space=pltpu.SMEM)] + [vmem] * len(pieces) + [hbm] * len(held),
        out_specs=[hbm, vmem],
        input_output_aliases={1 + len(pieces): 0} if held else {},
        scratch_shapes=[pltpu.VMEM((2, D, 2 * w), F32), pltpu.SemaphoreType.DMA((CHUNKS, 2))],
        compiler_params=pltpu.CompilerParams(vmem_limit_bytes=VMEM_BYTES),
        cost_estimate=pl.CostEstimate(flops=0, bytes_accessed=0, transcendentals=0),
    )(where, *pieces, *held)


def solution(mesh):
    return jax.shard_map(
        body,
        mesh=mesh,
        in_specs=(
            P(("grp", "seq", "rep"), None),
            P(),
            P(None, None, "head"),
            P("head", None),
            P(("grp", "seq", "rep"), None),
            P(("grp", "seq", "rep"), None),
        ),
        out_specs=(
            P(("grp", "seq", "rep"), None),
            P(("grp", "seq", "rep"), None),
            P("grp", None, "head"),
            P(("grp", "head"), None),
            P("grp"),
        ),
        check_vma=False,
    )
```

```python
import functools

import jax
import jax.numpy as jnp
from jax import lax
from jax.experimental import pallas as pl
from jax.experimental.pallas import tpu as pltpu
from jax.sharding import PartitionSpec as P

D = 512
E = 64
BLOCK = 512
CHUNKS = 4
MASK_ROWS = 16
GAIN_ROWS = 16
TOP = 320
LANES = 128
F32 = jnp.float32
BF16 = jnp.bfloat16
VMEM_BYTES = 16 * 1024 * 1024


def dot_nt(a, b):
    return lax.dot_general(a, b, (((1,), (1,)), ((), ())), preferred_element_type=F32)


def dot_tn(a, b):
    return lax.dot_general(a, b, (((0,), (0,)), ((), ())), preferred_element_type=F32)


def dot_nn(a, b):
    return lax.dot_general(a, b, (((1,), (0,)), ((), ())), preferred_element_type=F32)


def sigmoid(x):
    return 0.5 * jnp.tanh(0.5 * x) + 0.5


def whole(shape):
    zeros = (0,) * len(shape)
    return pl.BlockSpec(shape, lambda *_: zeros)


def call(kernel, out_shapes, args, scalars=(), us=0.0, fetched=0):
    n_scalars, n_out = len(scalars), len(out_shapes)

    def with_fetch(*refs):
        head, held, rest = refs[:n_scalars], refs[n_scalars : n_scalars + fetched], refs[n_scalars + fetched :]
        n_rest = len(args) - fetched + n_out
        slots, sems = rest[n_rest : n_rest + fetched], rest[n_rest + fetched]
        copies = [pltpu.make_async_copy(h, slot, sems.at[i]) for i, (h, slot) in enumerate(zip(held, slots))]
        for copy in copies:
            copy.start()

        def fetch(*which):
            for i in which:
                copies[i].wait()

        kernel(*head, *slots, *rest[:n_rest], fetch)

    scratch = [pltpu.VMEM(a.shape, a.dtype) for a in args[:fetched]]
    return pl.pallas_call(
        with_fetch if fetched else kernel,
        out_shape=out_shapes,
        in_specs=[pl.BlockSpec(memory_space=pltpu.SMEM)] * n_scalars
        + [pl.BlockSpec(memory_space=pltpu.HBM)] * fetched
        + [pl.BlockSpec(memory_space=pltpu.VMEM)] * (len(args) - fetched),
        out_specs=[pl.BlockSpec(memory_space=pltpu.VMEM)] * n_out,
        scratch_shapes=scratch + [pltpu.SemaphoreType.DMA((fetched,))] if fetched else [],
        compiler_params=pltpu.CompilerParams(vmem_limit_bytes=VMEM_BYTES),
        cost_estimate=pl.CostEstimate(flops=int(us * 1.1e9), bytes_accessed=0, transcendentals=0),
    )(*scalars, *args)


def shape(dims, dtype):
    return jax.ShapeDtypeStruct(dims, dtype)


def mask_at(where, mask_own, mask_oth, slot, col):
    at = jnp.where(where[1] == 1, col, 3 - col)
    return jnp.where(where[0] == slot, mask_own[0, at], mask_oth[0, at])


def slots(where):
    mine = where[0]
    return [pl.ds(pl.multiple_of(slot * BLOCK, BLOCK), BLOCK) for slot in (mine, 1 - mine)]


def project_kv_kernel(where, ev_own, ev_oth, w4, gain, normed, inv, slope, kv, fetch):
    fetch(0, 2)
    w_kv = jnp.concatenate([w4[2], w4[3]], axis=1)
    for i, (rows, events) in enumerate(zip(slots(where), (ev_own, ev_oth))):
        if i == 1:
            fetch(1)
        x = events[...].astype(F32)
        inverse = lax.rsqrt(jnp.mean(x * x, axis=1, keepdims=True) + 1e-06)
        n = (x * inverse * gain[...]).astype(BF16)
        normed[rows, :] = n
        inv[rows, :] = jnp.broadcast_to(inverse, (BLOCK, LANES))
        p = dot_nn(n, w_kv)
        s = sigmoid(p)
        slope[rows, :] = s * (1.0 + p * (1.0 - s))
        kv[rows, :] = (p * s).astype(BF16)


def project_gq_kernel(where, mask_own, mask_oth, cot_own, cot_oth, w4, ow, normed, slope, qa, gate, gm, fetch):
    w = w4.shape[2]
    fetch(0, 2, 3)
    w_gq = jnp.concatenate([w4[0], w4[1]], axis=1)
    wow = ow[pl.ds(pl.multiple_of(where[3] * w, w), w), :]
    for i, (rows, cot) in enumerate(zip(slots(where), (cot_own, cot_oth))):
        if i == 1:
            fetch(1)
        p = dot_nn(normed[rows, :], w_gq)
        s = sigmoid(p)
        slope[rows, :] = s * (1.0 + p * (1.0 - s))
        act = (p * s).astype(BF16)
        g = act[:, :w]
        gate[rows, :] = g
        grad_mixed = dot_nt(cot[...], wow)
        gm[rows, :] = grad_mixed
        qa[rows, :w] = act[:, w:]
        qa[rows, w:] = (grad_mixed * g.astype(F32)).astype(BF16)
    lane = lax.broadcasted_iota(jnp.int32, (MASK_ROWS, 2 * w), 1)
    marks = jnp.zeros((MASK_ROWS, 2 * w), F32)
    for slot in range(2):
        for col in range(4):
            m = mask_at(where, mask_own, mask_oth, slot, col).astype(F32)
            marks = jnp.where(lane == 4 * slot + col, m, marks)
    qa[2 * BLOCK :, :] = marks.astype(BF16)


TILE = 512


def block_rows(slot):
    return pl.ds(pl.multiple_of(slot * BLOCK, BLOCK), BLOCK)


def pair_side(left, l_slot, right, r_slot, acc):
    w = left.shape[1] // 2
    rows, r_rows = block_rows(l_slot), block_rows(r_slot)
    xr, yr = right[r_rows, :w], right[r_rows, w:]
    lane = lax.broadcasted_iota(jnp.int32, (1, w), 1) // E
    zero = jnp.zeros_like(xr)
    x = left[rows, :w] * jnp.asarray(0.5, BF16)
    y = left[rows, w:]
    acc_x = acc[rows, :w]
    acc_y = acc[rows, w:]
    for h in range(w // E):
        on = lane == h
        xh, yh = jnp.where(on, xr, zero), jnp.where(on, yr, zero)
        u = dot_nt(x, xh)
        g = dot_nt(y, yh)
        a = 1.0 + jnp.tanh(u)
        m = u * a
        slope = a + m * (2.0 - a)
        acc_y = acc_y + dot_nn(m.astype(BF16), yh)
        acc_x = acc_x + dot_nn((g * slope).astype(BF16), xh)
    acc[rows, :w] = acc_x
    acc[rows, w:] = acc_y


def pair_both(qa, q_slot, kv, k_slot, acc_q, acc_k):
    w = qa.shape[1] // 2
    k_rows = block_rows(k_slot)
    k, v = kv[k_rows, :w], kv[k_rows, w:]
    lane = lax.broadcasted_iota(jnp.int32, (1, w), 1) // E
    zero = jnp.zeros_like(k)
    grad_k, grad_v = acc_k[k_rows, :w], acc_k[k_rows, w:]
    for t in range(BLOCK // TILE):
        rows = pl.ds(pl.multiple_of(q_slot * BLOCK + t * TILE, TILE), TILE)
        q = qa[rows, :w] * jnp.asarray(0.5, BF16)
        ga = qa[rows, w:]
        acc_x = acc_q[rows, :w]
        acc_y = acc_q[rows, w:]
        for h in range(w // E):
            on = lane == h
            kh, vh = jnp.where(on, k, zero), jnp.where(on, v, zero)
            u = dot_nt(q, kh)
            a = 1.0 + jnp.tanh(u)
            m = u * a
            slope = a + m * (2.0 - a)
            weights = m.astype(BF16)
            grad_s = (dot_nt(ga, vh) * slope).astype(BF16)
            acc_y = acc_y + dot_nn(weights, vh)
            acc_x = acc_x + dot_nn(grad_s, kh)
            grad_k = grad_k + 2.0 * dot_tn(grad_s, jnp.where(on, q, jnp.zeros_like(q)))
            grad_v = grad_v + dot_tn(weights, jnp.where(on, ga, jnp.zeros_like(ga)))
        acc_q[rows, :w] = acc_x
        acc_q[rows, w:] = acc_y
    acc_k[k_rows, :w] = grad_k
    acc_k[k_rows, w:] = grad_v


def remote_pair(t, odd):
    q_slot, k_slot = (t == 1).astype(jnp.int32), (t == 2).astype(jnp.int32)
    col = 2 + (t > 0).astype(jnp.int32)
    return (1 - q_slot, 1 - k_slot, 3 - col) if odd else (q_slot, k_slot, col)


def loop(count, step):
    lax.fori_loop(0, count, lambda t, _: (step(t), 0)[1], 0)


def query_kernel(odd, where, mask_own, mask_oth, qa, kv, acc):
    acc[...] = jnp.zeros_like(acc)

    def step(t):
        q_slot, k_slot, col = remote_pair(t, odd)

        @pl.when(mask_at(where, mask_own, mask_oth, q_slot, col) == 1)
        def _():
            pair_side(qa, q_slot, kv, k_slot, acc)

    loop(3, step)


def key_kernel(odd, where, kv, qa, acc):
    acc[...] = jnp.zeros_like(acc)
    marks = qa[2 * BLOCK :, :].astype(F32)
    row = lax.broadcasted_iota(jnp.int32, marks.shape, 0)
    lane = lax.broadcasted_iota(jnp.int32, marks.shape, 1)

    def step(t):
        q_slot, k_slot, col = remote_pair(t, odd)
        m = jnp.sum(jnp.where((row == 0) & (lane == 4 * q_slot + col), marks, 0.0))
        on = m > 0.5
        if odd:
            on = on & (where[2] == 0)

        @pl.when(on)
        def _():
            pair_side(kv, k_slot, qa, q_slot, acc)

    loop(3, step)


def own_kernel(where, mask_own, mask_oth, qa, kv, normed, acc_q, acc_k, normed_t):
    normed_t[...] = normed[...].T
    acc_q[...] = jnp.zeros_like(acc_q)
    acc_k[...] = jnp.zeros_like(acc_k)

    def step(t):
        q_slot = t % 2
        k_slot = ((t == 1) | (t == 2)).astype(jnp.int32)
        masked = mask_at(where, mask_own, mask_oth, q_slot, jnp.maximum(t - 1, 0))

        @pl.when((t < 2) | (masked == 1))
        def _():
            pair_both(qa, q_slot, kv, k_slot, acc_q, acc_k)

    loop(4, step)


def query_finish_kernel(where, cot_own, cot_oth, gate, gm, slopes, normed_t, acc_a, acc_b, acc_c, mix_own, mix_oth, gp, packed):
    w = gate.shape[1]
    grad_out = jnp.zeros((w, D), F32)
    for rows, cot, mixed in zip(slots(where), (cot_own, cot_oth), (mix_own, mix_oth)):
        total = acc_a[rows, :] + acc_b[rows, :] + acc_c[rows, :]
        grad_query = total[:, :w] * (1.0 / 1024)
        attended = total[:, w:] * (1.0 / 512)
        mix = (attended * gate[rows, :].astype(F32)).astype(BF16)
        mixed[...] = mix
        slope = slopes[rows, :]
        gp[rows, :w] = (gm[rows, :] * attended * slope[:, :w]).astype(BF16)
        gp[rows, w:] = (grad_query * slope[:, w:]).astype(BF16)
        grad_out = grad_out + dot_tn(mix, cot[...])
    pack(packed, dot_nn(normed_t[...], gp[...]), grad_out)


def pack(packed, grad_in, grad_out=None):
    step = D // CHUNKS
    w = grad_in.shape[1] // 2
    for c in range(CHUNKS):
        for p in range(2):
            packed[c, p * step : (p + 1) * step, :] = grad_in[c * step : (c + 1) * step, p * w : (p + 1) * w].astype(BF16)
        if grad_out is not None:
            n = w // CHUNKS
            part = grad_out[c * n : (c + 1) * n].astype(BF16)
            for j in range(D // w):
                packed[c, 2 * step + j * n : 2 * step + (j + 1) * n, :] = part[:, j * w : (j + 1) * w]


def key_finish_kernel(
    where, ev_own, ev_oth, inv, slopes, normed_t, gp_gq, w4, acc_a, acc_b, acc_c, packed, gn_own, gn_oth, gp
):
    w = slopes.shape[1] // 2
    w_gq = jnp.concatenate([w4[0], w4[1]], axis=1)
    w_kv = jnp.concatenate([w4[2], w4[3]], axis=1)
    gain = jnp.zeros((1, D), F32)
    for rows, events, out in zip(slots(where), (ev_own, ev_oth), (gn_own, gn_oth)):
        total = acc_a[rows, :] + acc_b[rows, :] + acc_c[rows, :]
        slope = slopes[rows, :]
        gp[rows, :w] = (total[:, :w] * (1.0 / 1024) * slope[:, :w]).astype(BF16)
        gp[rows, w:] = (total[:, w:] * (1.0 / 512) * slope[:, w:]).astype(BF16)
        gn = dot_nt(gp_gq[rows, :], w_gq) + dot_nt(gp[rows, :], w_kv)
        out[...] = gn.astype(BF16)
        inverse = jnp.concatenate([inv[rows, :]] * (D // LANES), axis=1)
        gain = gain + jnp.sum(gn * events[...].astype(F32) * inverse, axis=0, keepdims=True)
    pack(packed, dot_nn(normed_t[...], gp[...]))
    high = gain.astype(BF16).astype(F32)
    parts = [v[:, j * w : (j + 1) * w] for v in (high, gain - high) for j in range(D // w)]
    if len(parts) < GAIN_ROWS:
        parts.append(jnp.zeros((GAIN_ROWS - len(parts), w), F32))
    for c in range(CHUNKS):
        packed[c, D // CHUNKS * 2 :, :] = jnp.concatenate(parts, axis=0).astype(BF16)


def add_cores_kernel(order, a, b, top, bottom):
    total = (a[...].astype(F32) + b[...].astype(F32)).astype(BF16)
    top[...] = total[:TOP]
    bottom[...] = total[TOP:]


def add_chunks_gain_kernel(order, *refs):
    pieces, (bottom, out, wide) = refs[:4], refs[4:]
    n, w = out.shape
    a, b, c, d = (piece[...].astype(F32) for piece in pieces)
    total = (a + b) + (c + d)
    out[...] = total[:n].astype(BF16)
    k = D // w
    rows = [total[n + j : n + j + 1] + total[n + k + j : n + k + j + 1] for j in range(k)]
    gain = jnp.concatenate(rows, axis=1)
    wide[: BLOCK - TOP, :] = bottom[...]
    wide[BLOCK - TOP :, :] = split_rows(gain)


def split_rows(total):
    high = total.astype(BF16).astype(F32)
    rest = jnp.zeros((GAIN_ROWS - 2, total.shape[1]), F32)
    return jnp.concatenate([high, total - high, rest], axis=0).astype(BF16)


def join_rows(rows):
    both = rows.astype(F32)
    return both[0:1] + both[1:2]


def add_chunks_kernel(order, a, b, c, d, out):
    out[...] = ((a[...].astype(F32) + b[...].astype(F32)) + (c[...].astype(F32) + d[...].astype(F32))).astype(BF16)


def assemble_kernel(first, where, *refs):
    pieces, rest = refs[:8], refs[8:]
    if first:
        pg_a, pg_b, _, grad_in, pg, parts, sem = rest
        pg[...] = pg_a[...] + pg_b[...]
    else:
        grad_in, grad_out, parts, sem = rest
    w = pieces[0].shape[1]
    step = D // CHUNKS
    n = w // CHUNKS

    def place(i, piece, core):
        lanes = slice(core * w, (core + 1) * w)
        rows = pl.ds(pl.multiple_of(where[4 + i] * step, step), step)
        for p in range(2):
            parts[p, rows, lanes] = piece[p * step : (p + 1) * step, :].astype(F32)
        if first == 0:
            for j in range(D // w):
                block = piece[2 * step + j * n : 2 * step + (j + 1) * n, :]
                out_rows = pl.ds(pl.multiple_of(core * w + where[4 + i] * n, n), n)
                grad_out[out_rows, j * w : (j + 1) * w] = block.astype(F32)

    def copy(i, p):
        rows = pl.ds(pl.multiple_of(where[4 + i] * step, step), step)
        return pltpu.make_async_copy(parts.at[p, rows], grad_in.at[rows, first + p], sem.at[i, p])

    for i in range(CHUNKS):
        for core in range(2):

            @pl.when(where[3] == core)
            def _():
                place(i, pieces[i], core)
                place(i, pieces[4 + i], 1 - core)

        for p in range(2):
            copy(i, p).start()
    for i in range(CHUNKS):
        for p in range(2):
            copy(i, p).wait()


def events_kernel(events, gain, top, bottom, top_x, bottom_x, grad, pg):
    for start, rows, mine, other in ((0, TOP, top, top_x), (TOP, BLOCK - TOP, bottom, bottom_x)):
        x = events[start : start + rows, :].astype(F32)
        inverse = lax.rsqrt(jnp.mean(x * x, axis=1, keepdims=True) + 1e-06)
        gn = mine[:rows, :].astype(F32) + other[:rows, :].astype(F32)
        scaled = gn * gain[...]
        mean = jnp.mean(scaled * x, axis=1, keepdims=True)
        grad[start : start + rows, :] = inverse * scaled - x * (inverse * inverse * inverse) * mean
    pg[...] = join_rows(bottom[BLOCK - TOP :, :]) + join_rows(bottom_x[BLOCK - TOP :, :])


def output_kernel(where, mine, rep, mine_x, rep_x, ow, ow_x, out):
    w = mine.shape[1]
    r = where[3]
    first = pl.ds(pl.multiple_of(r * w, w), w)
    second = pl.ds(pl.multiple_of((1 - r) * w, w), w)
    here = dot_nn(mine[...], ow[first, :]) + dot_nn(rep[...], ow[second, :])
    there = dot_nn(mine_x[...], ow_x[first, :]) + dot_nn(rep_x[...], ow_x[second, :])
    out[...] = (here + there).astype(BF16)


def swap(x, axis, bit=1):
    n = lax.axis_size(axis)
    return lax.ppermute(x, axis, [(i, i ^ bit) for i in range(n)])


def route_even(n):
    return [(2 * i + r, 2 * (i ^ 1) + r) for i in range(n) for r in range(2)]


def route_odd(n):
    route = []
    for i in range(n):
        for r in range(2):
            if i in (0, n - 1):
                route.append((2 * i + r, 2 * i + 1 - r))
            else:
                route.append((2 * i + r, 2 * (((i - 1) ^ 1) + 1) + r))
    return route


def scatter_over_seq(packed):
    me = lax.axis_index("seq")

    def chunk(d):
        return lax.dynamic_index_in_dim(packed, me ^ d, 0, keepdims=False)

    return [chunk(0)] + [swap(chunk(d), "seq", d) for d in (1, 2, 3)]


def gather_over_seq(total):
    return [total] + [swap(total, "seq", d) for d in (1, 2, 3)]


def after(values, *others):
    return lax.optimization_barrier((values, others))[0]


def body(events, norm_gain, in_weight, out_weight, pair_mask, cotangent):
    n_seq, n_head = lax.axis_size("seq"), lax.axis_size("head")
    direct = n_seq == CHUNKS and n_head == 2
    rep, seq = lax.axis_index("rep"), lax.axis_index("seq")
    w = in_weight.shape[2] // 2
    rows2 = 2 * BLOCK
    step = D // CHUNKS
    flip = 1 - seq % 2
    edge = ((seq == 0) | (seq == n_seq - 1)).astype(jnp.int32)
    chunk_ids = [(seq ^ d) if direct else jnp.int32(d) for d in range(CHUNKS)]
    where = jnp.stack([rep ^ flip, flip, edge, rep] + chunk_ids).astype(jnp.int32)

    ev_oth = swap(events, "rep")
    cot_oth = swap(cotangent, "rep")
    mask_oth = swap(pair_mask, "rep")
    scalars = [where, pair_mask, mask_oth]
    gain = norm_gain.reshape(1, D)
    w4 = lax.dynamic_slice(in_weight, (0, 0, rep * w), (D, 4, w)).transpose(1, 0, 2)
    axes = ("seq", "rep")
    even, odd = route_even(n_seq), route_odd(n_seq)

    normed, inv, slope_kv, kv = call(
        project_kv_kernel,
        [shape((rows2, D), BF16), shape((rows2, LANES), F32), shape((rows2, 2 * w), F32), shape((rows2, 2 * w), BF16)],
        [events, ev_oth, w4, gain],
        [where],
        fetched=3,
    )
    kv_even = lax.ppermute(kv, axes, even)
    kv_odd = lax.ppermute(kv, axes, odd)
    slope_gq, qa, gate, gm = call(
        project_gq_kernel,
        [
            shape((rows2, 2 * w), F32),
            shape((rows2 + MASK_ROWS, 2 * w), BF16),
            shape((rows2, w), BF16),
            shape((rows2, w), F32),
        ],
        [cotangent, cot_oth, w4, out_weight, normed],
        scalars,
        fetched=4,
    )
    qa_even = lax.ppermute(qa, axes, even)
    qa_odd = lax.ppermute(qa, axes, odd)
    acc_shape = shape((rows2, 2 * w), F32)
    q_own, k_own, normed_t = call(
        own_kernel, [acc_shape, acc_shape, shape((D, rows2), BF16)], [qa, kv, normed], scalars, us=9
    )
    (q_even,) = call(functools.partial(query_kernel, False), [acc_shape], [qa, kv_even], scalars, us=5)
    late = where
    if n_head == 2:
        ow_x = swap(out_weight, "head")
        late = after(where, ow_x, q_even)
    (q_odd,) = call(
        functools.partial(query_kernel, True), [acc_shape], [qa, kv_odd], [late, pair_mask, mask_oth], us=5
    )
    mix_own, mix_oth, gp_gq, pack_q = call(
        query_finish_kernel,
        [
            shape((BLOCK, w), BF16),
            shape((BLOCK, w), BF16),
            shape((rows2, 2 * w), BF16),
            shape((CHUNKS, 2 * step + D // CHUNKS, w), BF16),
        ],
        [cotangent, cot_oth, gate, gm, slope_gq, normed_t, q_own, q_even, q_odd],
        [where],
    )
    mix_rep = swap(mix_oth, "rep")
    (k_far,) = call(functools.partial(key_kernel, False), [acc_shape], [kv, qa_even], [where], us=6)
    add_shape = shape((2 * step + D // CHUNKS, w), BF16)
    if direct:
        mixed_x = [swap(mix_own, "head"), swap(mix_rep, "head")]
        got_q = scatter_over_seq(pack_q)
        late = after(where, k_far, got_q)
        (sum_q,) = call(add_chunks_kernel, [add_shape], got_q, [where])
        all_q = gather_over_seq(sum_q)
    else:
        mixed_x = []
        late = where
        sums = lax.psum(pack_q.astype(F32), "seq").astype(BF16)
        all_q = [sums[i] for i in range(CHUNKS)]
    (k_last,) = call(functools.partial(key_kernel, True), [acc_shape], [kv, qa_odd], [late], us=6)
    oth_q = [swap(piece, "rep") for piece in all_q]
    last = after(where, k_last, mixed_x, all_q)

    pack_kv, gn_own, gn_oth, _ = call(
        key_finish_kernel,
        [
            shape((CHUNKS, 2 * step + GAIN_ROWS, w), BF16),
            shape((BLOCK, D), BF16),
            shape((BLOCK, D), BF16),
            shape((rows2, 2 * w), BF16),
        ],
        [events, ev_oth, inv, slope_kv, normed_t, gp_gq, w4, k_own, k_far, k_last],
        [last],
    )
    late = where
    if direct:
        got_kv = scatter_over_seq(pack_kv)
    halves = [shape((TOP, D), BF16), shape((BLOCK - TOP, D), BF16)]
    top, bottom = call(add_cores_kernel, halves, [gn_own, swap(gn_oth, "rep")], [late])
    if n_head == 2:
        (output,) = call(
            output_kernel,
            [shape((BLOCK, D), BF16)],
            [mix_own, mix_rep, *(mixed_x or [swap(mix_own, "head"), swap(mix_rep, "head")]), out_weight, ow_x],
            [where],
        )
        top_x = swap(top, "head")
    else:
        weight = jnp.where(rep == 0, out_weight, jnp.roll(out_weight, w, axis=0))
        mixed = jnp.concatenate([mix_own, mix_rep], axis=1)
        output = lax.psum(dot_nn(mixed, weight), "head").astype(BF16)
        top, bottom = lax.psum((top.astype(F32), bottom.astype(F32)), "head")
        top_x = jnp.zeros_like(top)
    wide = shape((BLOCK - TOP + GAIN_ROWS, D), BF16)
    if direct:
        sum_kv, bottom = call(
            add_chunks_gain_kernel,
            [shape((2 * step, w), BF16), wide],
            [*got_kv, bottom],
            [after(where, output, oth_q)],
        )
        bottom_x = swap(bottom, "head")
        all_kv = gather_over_seq(sum_kv)
    else:
        sums = lax.psum(pack_kv.astype(F32), "seq")
        all_kv = [sums[i, : 2 * step].astype(BF16) for i in range(CHUNKS)]
        pg = sums[0, 2 * step :]
        pg = (pg[: D // w] + pg[D // w : 2 * (D // w)]).reshape(1, D)
        pg = jnp.concatenate([pg, jnp.zeros((GAIN_ROWS - 1, D), F32)])
        bottom, bottom_x = jnp.concatenate([bottom, lax.psum(pg, "head")]), jnp.zeros(wide.shape, F32)
    grad_events, pg = call(
        events_kernel,
        [shape((BLOCK, D), F32), shape((1, D), F32)],
        [events, gain, top, bottom, top_x, bottom_x],
    )
    grad_in, grad_out = assemble(late, [*all_q, *oth_q], w)
    all_kv = after(all_kv, grad_out, pg)
    oth_kv = [swap(piece, "rep") for piece in all_kv]
    grad_in, pg = assemble(where, [*all_kv, *oth_kv, pg, swap(pg, "rep")], w, grad_in)
    return (output, grad_events, grad_in, grad_out, pg.reshape(D))


def assemble(where, pieces, w, grad_in=None):
    held = [] if grad_in is None else [grad_in]
    hbm, vmem = pl.BlockSpec(memory_space=pltpu.HBM), pl.BlockSpec(memory_space=pltpu.VMEM)
    return pl.pallas_call(
        functools.partial(assemble_kernel, 2 * len(held)),
        out_shape=[shape((D, 4, 2 * w), F32), shape((1, D) if held else (2 * w, D), F32)],
        in_specs=[pl.BlockSpec(memory_space=pltpu.SMEM)] + [vmem] * len(pieces) + [hbm] * len(held),
        out_specs=[hbm, vmem],
        input_output_aliases={1 + len(pieces): 0} if held else {},
        scratch_shapes=[pltpu.VMEM((2, D, 2 * w), F32), pltpu.SemaphoreType.DMA((CHUNKS, 2))],
        compiler_params=pltpu.CompilerParams(vmem_limit_bytes=VMEM_BYTES),
        cost_estimate=pl.CostEstimate(flops=0, bytes_accessed=0, transcendentals=0),
    )(where, *pieces, *held)


def solution(mesh):
    return jax.shard_map(
        body,
        mesh=mesh,
        in_specs=(
            P(("grp", "seq", "rep"), None),
            P(),
            P(None, None, "head"),
            P("head", None),
            P(("grp", "seq", "rep"), None),
            P(("grp", "seq", "rep"), None),
        ),
        out_specs=(
            P(("grp", "seq", "rep"), None),
            P(("grp", "seq", "rep"), None),
            P("grp", None, "head"),
            P(("grp", "head"), None),
            P("grp"),
        ),
        check_vma=False,
    )
```

```python
import functools

import jax
import jax.numpy as jnp
from jax import lax
from jax.experimental import pallas as pl
from jax.experimental.pallas import tpu as pltpu
from jax.sharding import PartitionSpec as P

D = 512
E = 64
BLOCK = 512
CHUNKS = 4
MASK_ROWS = 16
GAIN_ROWS = 16
LANES = 128
F32 = jnp.float32
BF16 = jnp.bfloat16
VMEM_BYTES = 16 * 1024 * 1024


def dot_nt(a, b):
    return lax.dot_general(a, b, (((1,), (1,)), ((), ())), preferred_element_type=F32)


def dot_tn(a, b):
    return lax.dot_general(a, b, (((0,), (0,)), ((), ())), preferred_element_type=F32)


def dot_nn(a, b):
    return lax.dot_general(a, b, (((1,), (0,)), ((), ())), preferred_element_type=F32)


def sigmoid(x):
    return 0.5 * jnp.tanh(0.5 * x) + 0.5


def whole(shape):
    zeros = (0,) * len(shape)
    return pl.BlockSpec(shape, lambda *_: zeros)


def call(kernel, out_shapes, args, scalars=(), us=0.0, fetched=0):
    n_scalars, n_out = len(scalars), len(out_shapes)

    def with_fetch(*refs):
        head, held, rest = refs[:n_scalars], refs[n_scalars : n_scalars + fetched], refs[n_scalars + fetched :]
        n_rest = len(args) - fetched + n_out
        slots, sems = rest[n_rest : n_rest + fetched], rest[n_rest + fetched]
        copies = [pltpu.make_async_copy(h, slot, sems.at[i]) for i, (h, slot) in enumerate(zip(held, slots))]
        for copy in copies:
            copy.start()

        def fetch(*which):
            for i in which:
                copies[i].wait()

        kernel(*head, *slots, *rest[:n_rest], fetch)

    scratch = [pltpu.VMEM(a.shape, a.dtype) for a in args[:fetched]]
    return pl.pallas_call(
        with_fetch if fetched else kernel,
        out_shape=out_shapes,
        in_specs=[pl.BlockSpec(memory_space=pltpu.SMEM)] * n_scalars
        + [pl.BlockSpec(memory_space=pltpu.HBM)] * fetched
        + [pl.BlockSpec(memory_space=pltpu.VMEM)] * (len(args) - fetched),
        out_specs=[pl.BlockSpec(memory_space=pltpu.VMEM)] * n_out,
        scratch_shapes=scratch + [pltpu.SemaphoreType.DMA((fetched,))] if fetched else [],
        compiler_params=pltpu.CompilerParams(vmem_limit_bytes=VMEM_BYTES),
        cost_estimate=pl.CostEstimate(flops=int(us * 1.1e9), bytes_accessed=0, transcendentals=0),
    )(*scalars, *args)


def shape(dims, dtype):
    return jax.ShapeDtypeStruct(dims, dtype)


def mask_at(where, mask_own, mask_oth, slot, col):
    at = jnp.where(where[1] == 1, col, 3 - col)
    return jnp.where(where[0] == slot, mask_own[0, at], mask_oth[0, at])


def slots(where):
    mine = where[0]
    return [pl.ds(pl.multiple_of(slot * BLOCK, BLOCK), BLOCK) for slot in (mine, 1 - mine)]


def project_kv_kernel(where, ev_own, ev_oth, w4, gain, normed, inv, slope, kv, fetch):
    fetch(0, 2)
    w_kv = jnp.concatenate([w4[2], w4[3]], axis=1)
    for i, (rows, events) in enumerate(zip(slots(where), (ev_own, ev_oth))):
        if i == 1:
            fetch(1)
        x = events[...].astype(F32)
        inverse = lax.rsqrt(jnp.mean(x * x, axis=1, keepdims=True) + 1e-06)
        n = (x * inverse * gain[...]).astype(BF16)
        normed[rows, :] = n
        inv[rows, :] = jnp.broadcast_to(inverse, (BLOCK, LANES))
        p = dot_nn(n, w_kv)
        s = sigmoid(p)
        slope[rows, :] = s * (1.0 + p * (1.0 - s))
        kv[rows, :] = (p * s).astype(BF16)


def project_gq_kernel(where, mask_own, mask_oth, cot_own, cot_oth, w4, ow, normed, slope, qa, gate, gm, fetch):
    w = w4.shape[2]
    fetch(0, 2, 3)
    w_gq = jnp.concatenate([w4[0], w4[1]], axis=1)
    wow = ow[pl.ds(pl.multiple_of(where[3] * w, w), w), :]
    for i, (rows, cot) in enumerate(zip(slots(where), (cot_own, cot_oth))):
        if i == 1:
            fetch(1)
        p = dot_nn(normed[rows, :], w_gq)
        s = sigmoid(p)
        slope[rows, :] = s * (1.0 + p * (1.0 - s))
        act = (p * s).astype(BF16)
        g = act[:, :w]
        gate[rows, :] = g
        grad_mixed = dot_nt(cot[...], wow)
        gm[rows, :] = grad_mixed
        qa[rows, :w] = act[:, w:]
        qa[rows, w:] = (grad_mixed * g.astype(F32)).astype(BF16)
    lane = lax.broadcasted_iota(jnp.int32, (MASK_ROWS, 2 * w), 1)
    marks = jnp.zeros((MASK_ROWS, 2 * w), F32)
    for slot in range(2):
        for col in range(4):
            m = mask_at(where, mask_own, mask_oth, slot, col).astype(F32)
            marks = jnp.where(lane == 4 * slot + col, m, marks)
    qa[2 * BLOCK :, :] = marks.astype(BF16)


TILE = 512


def block_rows(slot):
    return pl.ds(pl.multiple_of(slot * BLOCK, BLOCK), BLOCK)


def pair_side(left, l_slot, right, r_slot, acc):
    w = left.shape[1] // 2
    rows, r_rows = block_rows(l_slot), block_rows(r_slot)
    xr, yr = right[r_rows, :w], right[r_rows, w:]
    lane = lax.broadcasted_iota(jnp.int32, (1, w), 1) // E
    zero = jnp.zeros_like(xr)
    x = left[rows, :w] * jnp.asarray(0.5, BF16)
    y = left[rows, w:]
    acc_x = acc[rows, :w]
    acc_y = acc[rows, w:]
    for h in range(w // E):
        on = lane == h
        xh, yh = jnp.where(on, xr, zero), jnp.where(on, yr, zero)
        u = dot_nt(x, xh)
        g = dot_nt(y, yh)
        a = 1.0 + jnp.tanh(u)
        m = u * a
        slope = a + m * (2.0 - a)
        acc_y = acc_y + dot_nn(m.astype(BF16), yh)
        acc_x = acc_x + dot_nn((g * slope).astype(BF16), xh)
    acc[rows, :w] = acc_x
    acc[rows, w:] = acc_y


def pair_both(qa, q_slot, kv, k_slot, acc_q, acc_k):
    w = qa.shape[1] // 2
    k_rows = block_rows(k_slot)
    k, v = kv[k_rows, :w], kv[k_rows, w:]
    lane = lax.broadcasted_iota(jnp.int32, (1, w), 1) // E
    zero = jnp.zeros_like(k)
    grad_k, grad_v = acc_k[k_rows, :w], acc_k[k_rows, w:]
    for t in range(BLOCK // TILE):
        rows = pl.ds(pl.multiple_of(q_slot * BLOCK + t * TILE, TILE), TILE)
        q = qa[rows, :w] * jnp.asarray(0.5, BF16)
        ga = qa[rows, w:]
        acc_x = acc_q[rows, :w]
        acc_y = acc_q[rows, w:]
        for h in range(w // E):
            on = lane == h
            kh, vh = jnp.where(on, k, zero), jnp.where(on, v, zero)
            u = dot_nt(q, kh)
            a = 1.0 + jnp.tanh(u)
            m = u * a
            slope = a + m * (2.0 - a)
            weights = m.astype(BF16)
            grad_s = (dot_nt(ga, vh) * slope).astype(BF16)
            acc_y = acc_y + dot_nn(weights, vh)
            acc_x = acc_x + dot_nn(grad_s, kh)
            grad_k = grad_k + 2.0 * dot_tn(grad_s, jnp.where(on, q, jnp.zeros_like(q)))
            grad_v = grad_v + dot_tn(weights, jnp.where(on, ga, jnp.zeros_like(ga)))
        acc_q[rows, :w] = acc_x
        acc_q[rows, w:] = acc_y
    acc_k[k_rows, :w] = grad_k
    acc_k[k_rows, w:] = grad_v


def remote_pair(t, odd):
    q_slot, k_slot = (t == 1).astype(jnp.int32), (t == 2).astype(jnp.int32)
    col = 2 + (t > 0).astype(jnp.int32)
    return (1 - q_slot, 1 - k_slot, 3 - col) if odd else (q_slot, k_slot, col)


def loop(count, step):
    lax.fori_loop(0, count, lambda t, _: (step(t), 0)[1], 0)


def query_kernel(odd, where, mask_own, mask_oth, qa, kv, acc):
    acc[...] = jnp.zeros_like(acc)

    def step(t):
        q_slot, k_slot, col = remote_pair(t, odd)

        @pl.when(mask_at(where, mask_own, mask_oth, q_slot, col) == 1)
        def _():
            pair_side(qa, q_slot, kv, k_slot, acc)

    loop(3, step)


def key_kernel(odd, where, kv, qa, acc):
    acc[...] = jnp.zeros_like(acc)
    marks = qa[2 * BLOCK :, :].astype(F32)
    row = lax.broadcasted_iota(jnp.int32, marks.shape, 0)
    lane = lax.broadcasted_iota(jnp.int32, marks.shape, 1)

    def step(t):
        q_slot, k_slot, col = remote_pair(t, odd)
        m = jnp.sum(jnp.where((row == 0) & (lane == 4 * q_slot + col), marks, 0.0))
        on = m > 0.5
        if odd:
            on = on & (where[2] == 0)

        @pl.when(on)
        def _():
            pair_side(kv, k_slot, qa, q_slot, acc)

    loop(3, step)


def own_kernel(where, mask_own, mask_oth, qa, kv, normed, acc_q, acc_k, normed_t):
    normed_t[...] = normed[...].T
    acc_q[...] = jnp.zeros_like(acc_q)
    acc_k[...] = jnp.zeros_like(acc_k)

    def step(t):
        q_slot = t % 2
        k_slot = ((t == 1) | (t == 2)).astype(jnp.int32)
        masked = mask_at(where, mask_own, mask_oth, q_slot, jnp.maximum(t - 1, 0))

        @pl.when((t < 2) | (masked == 1))
        def _():
            pair_both(qa, q_slot, kv, k_slot, acc_q, acc_k)

    loop(4, step)


def query_finish_kernel(where, cot_own, cot_oth, gate, gm, slopes, normed_t, acc_a, acc_b, acc_c, mix_own, mix_oth, gp, packed):
    w = gate.shape[1]
    grad_out = jnp.zeros((w, D), F32)
    for rows, cot, mixed in zip(slots(where), (cot_own, cot_oth), (mix_own, mix_oth)):
        total = acc_a[rows, :] + acc_b[rows, :] + acc_c[rows, :]
        grad_query = total[:, :w] * (1.0 / 1024)
        attended = total[:, w:] * (1.0 / 512)
        mix = (attended * gate[rows, :].astype(F32)).astype(BF16)
        mixed[...] = mix
        slope = slopes[rows, :]
        gp[rows, :w] = (gm[rows, :] * attended * slope[:, :w]).astype(BF16)
        gp[rows, w:] = (grad_query * slope[:, w:]).astype(BF16)
        grad_out = grad_out + dot_tn(mix, cot[...])
    pack(packed, dot_nn(normed_t[...], gp[...]), grad_out)


def pack(packed, grad_in, grad_out=None):
    step = D // CHUNKS
    w = grad_in.shape[1] // 2
    for c in range(CHUNKS):
        for p in range(2):
            packed[c, p * step : (p + 1) * step, :] = grad_in[c * step : (c + 1) * step, p * w : (p + 1) * w].astype(BF16)
        if grad_out is not None:
            n = w // CHUNKS
            part = grad_out[c * n : (c + 1) * n].astype(BF16)
            for j in range(D // w):
                packed[c, 2 * step + j * n : 2 * step + (j + 1) * n, :] = part[:, j * w : (j + 1) * w]


def grad_normed_kernel(
    where, ev_own, ev_oth, inv, slopes, gp_gq, w4, acc_a, acc_b, acc_c, gn_own, gn_oth, gp, gain
):
    w = slopes.shape[1] // 2
    w_gq = jnp.concatenate([w4[0], w4[1]], axis=1)
    w_kv = jnp.concatenate([w4[2], w4[3]], axis=1)
    share = jnp.zeros((1, D), F32)
    for rows, events, out in zip(slots(where), (ev_own, ev_oth), (gn_own, gn_oth)):
        total = acc_a[rows, :] + acc_b[rows, :] + acc_c[rows, :]
        slope = slopes[rows, :]
        gp[rows, :w] = (total[:, :w] * (1.0 / 1024) * slope[:, :w]).astype(BF16)
        gp[rows, w:] = (total[:, w:] * (1.0 / 512) * slope[:, w:]).astype(BF16)
        gn = dot_nt(gp_gq[rows, :], w_gq) + dot_nt(gp[rows, :], w_kv)
        out[...] = gn.astype(BF16)
        inverse = jnp.concatenate([inv[rows, :]] * (D // LANES), axis=1)
        share = share + jnp.sum(gn * events[...].astype(F32) * inverse, axis=0, keepdims=True)
    gain[...] = share


def key_weights_kernel(normed_t, gp, gain, packed):
    w = gp.shape[1] // 2
    pack(packed, dot_nn(normed_t[...], gp[...]))
    share = gain[...]
    high = share.astype(BF16).astype(F32)
    parts = [v[:, j * w : (j + 1) * w] for v in (high, share - high) for j in range(D // w)]
    if len(parts) < GAIN_ROWS:
        parts.append(jnp.zeros((GAIN_ROWS - len(parts), w), F32))
    for c in range(CHUNKS):
        packed[c, D // CHUNKS * 2 :, :] = jnp.concatenate(parts, axis=0).astype(BF16)


def add_cores_kernel(order, a, b, out):
    out[...] = (a[...].astype(F32) + b[...].astype(F32)).astype(BF16)


def add_chunks_gain_kernel(order, *refs):
    pieces, (out, gain) = refs[:4], refs[4:]
    n, w = out.shape
    a, b, c, d = (piece[...].astype(F32) for piece in pieces)
    total = (a + b) + (c + d)
    out[...] = total[:n].astype(BF16)
    k = D // w
    for j in range(k):
        gain[:, j * w : (j + 1) * w] = total[n + j : n + j + 1] + total[n + k + j : n + k + j + 1]


def add_chunks_kernel(order, a, b, c, d, out):
    out[...] = ((a[...].astype(F32) + b[...].astype(F32)) + (c[...].astype(F32) + d[...].astype(F32))).astype(BF16)


def assemble_kernel(first, where, *refs):
    if first:
        pieces, (pg_a, pg_b, _, grad_in, pg, parts, sem) = refs[:8], refs[8:]
        pg[...] = pg_a[...] + pg_b[...]
    else:
        both, (grad_in, grad_out, parts, sem) = refs[:2], refs[2:]
        n = both[0].shape[0] // CHUNKS
        pieces = [held.at[pl.ds(i * n, n)] for held in both for i in range(CHUNKS)]
    w = pieces[0].shape[1]
    step = D // CHUNKS
    n = w // CHUNKS

    def place(i, piece, core):
        lanes = slice(core * w, (core + 1) * w)
        rows = pl.ds(pl.multiple_of(where[4 + i] * step, step), step)
        for p in range(2):
            parts[p, rows, lanes] = piece[p * step : (p + 1) * step, :].astype(F32)
        if first == 0:
            for j in range(D // w):
                block = piece[2 * step + j * n : 2 * step + (j + 1) * n, :]
                out_rows = pl.ds(pl.multiple_of(core * w + where[4 + i] * n, n), n)
                grad_out[out_rows, j * w : (j + 1) * w] = block.astype(F32)

    def copy(i, p):
        rows = pl.ds(pl.multiple_of(where[4 + i] * step, step), step)
        return pltpu.make_async_copy(parts.at[p, rows], grad_in.at[rows, first + p], sem.at[i, p])

    for i in range(CHUNKS):
        for core in range(2):

            @pl.when(where[3] == core)
            def _():
                place(i, pieces[i], core)
                place(i, pieces[4 + i], 1 - core)

        for p in range(2):
            copy(i, p).start()
    for i in range(CHUNKS):
        for p in range(2):
            copy(i, p).wait()


def events_kernel(order, events, gain, mine, other, pg_a, pg_b, grad, pg):
    x = events[...].astype(F32)
    inverse = lax.rsqrt(jnp.mean(x * x, axis=1, keepdims=True) + 1e-06)
    gn = mine[...].astype(F32) + other[...].astype(F32)
    scaled = gn * gain[...]
    mean = jnp.mean(scaled * x, axis=1, keepdims=True)
    grad[...] = inverse * scaled - x * (inverse * inverse * inverse) * mean
    pg[...] = pg_a[...] + pg_b[...]


def output_kernel(where, mine, rep, mine_x, rep_x, ow, ow_x, out):
    w = mine.shape[1]
    r = where[3]
    first = pl.ds(pl.multiple_of(r * w, w), w)
    second = pl.ds(pl.multiple_of((1 - r) * w, w), w)
    here = dot_nn(mine[...], ow[first, :]) + dot_nn(rep[...], ow[second, :])
    there = dot_nn(mine_x[...], ow_x[first, :]) + dot_nn(rep_x[...], ow_x[second, :])
    out[...] = (here + there).astype(BF16)


def swap(x, axis, bit=1):
    n = lax.axis_size(axis)
    return lax.ppermute(x, axis, [(i, i ^ bit) for i in range(n)])


def route_even(n):
    return [(2 * i + r, 2 * (i ^ 1) + r) for i in range(n) for r in range(2)]


def route_odd(n):
    route = []
    for i in range(n):
        for r in range(2):
            if i in (0, n - 1):
                route.append((2 * i + r, 2 * i + 1 - r))
            else:
                route.append((2 * i + r, 2 * (((i - 1) ^ 1) + 1) + r))
    return route


def scatter_over_seq(packed):
    me = lax.axis_index("seq")

    def chunk(d):
        return lax.dynamic_index_in_dim(packed, me ^ d, 0, keepdims=False)

    return [chunk(0)] + [swap(chunk(d), "seq", d) for d in (1, 2, 3)]


def gather_over_seq(total):
    return [total] + [swap(total, "seq", d) for d in (1, 2, 3)]


def after(values, *others):
    return lax.optimization_barrier((values, others))[0]


def body(events, norm_gain, in_weight, out_weight, pair_mask, cotangent):
    n_seq, n_head = lax.axis_size("seq"), lax.axis_size("head")
    direct = n_seq == CHUNKS and n_head == 2
    rep, seq = lax.axis_index("rep"), lax.axis_index("seq")
    w = in_weight.shape[2] // 2
    rows2 = 2 * BLOCK
    step = D // CHUNKS
    flip = 1 - seq % 2
    edge = ((seq == 0) | (seq == n_seq - 1)).astype(jnp.int32)
    chunk_ids = [(seq ^ d) if direct else jnp.int32(d) for d in range(CHUNKS)]
    where = jnp.stack([rep ^ flip, flip, edge, rep] + chunk_ids).astype(jnp.int32)

    ev_oth = swap(events, "rep")
    cot_oth = swap(cotangent, "rep")
    mask_oth = swap(pair_mask, "rep")
    scalars = [where, pair_mask, mask_oth]
    gain = norm_gain.reshape(1, D)
    w4 = lax.dynamic_slice(in_weight, (0, 0, rep * w), (D, 4, w)).transpose(1, 0, 2)
    axes = ("seq", "rep")
    even, odd = route_even(n_seq), route_odd(n_seq)

    normed, inv, slope_kv, kv = call(
        project_kv_kernel,
        [shape((rows2, D), BF16), shape((rows2, LANES), F32), shape((rows2, 2 * w), F32), shape((rows2, 2 * w), BF16)],
        [events, ev_oth, w4, gain],
        [where],
        fetched=3,
    )
    kv_even = lax.ppermute(kv, axes, even)
    kv_odd = lax.ppermute(kv, axes, odd)
    slope_gq, qa, gate, gm = call(
        project_gq_kernel,
        [
            shape((rows2, 2 * w), F32),
            shape((rows2 + MASK_ROWS, 2 * w), BF16),
            shape((rows2, w), BF16),
            shape((rows2, w), F32),
        ],
        [cotangent, cot_oth, w4, out_weight, normed],
        scalars,
        fetched=4,
    )
    qa_even = lax.ppermute(qa, axes, even)
    qa_odd = lax.ppermute(qa, axes, odd)
    acc_shape = shape((rows2, 2 * w), F32)
    q_own, k_own, normed_t = call(
        own_kernel, [acc_shape, acc_shape, shape((D, rows2), BF16)], [qa, kv, normed], scalars, us=9
    )
    (q_even,) = call(functools.partial(query_kernel, False), [acc_shape], [qa, kv_even], scalars, us=5)
    late = where
    if n_head == 2:
        ow_x = swap(out_weight, "head")
        late = after(where, ow_x, q_even)
    (q_odd,) = call(
        functools.partial(query_kernel, True), [acc_shape], [qa, kv_odd], [late, pair_mask, mask_oth], us=5
    )
    mix_own, mix_oth, gp_gq, pack_q = call(
        query_finish_kernel,
        [
            shape((BLOCK, w), BF16),
            shape((BLOCK, w), BF16),
            shape((rows2, 2 * w), BF16),
            shape((CHUNKS, 2 * step + D // CHUNKS, w), BF16),
        ],
        [cotangent, cot_oth, gate, gm, slope_gq, normed_t, q_own, q_even, q_odd],
        [where],
    )
    mix_rep = swap(mix_oth, "rep")
    (k_far,) = call(functools.partial(key_kernel, False), [acc_shape], [kv, qa_even], [where], us=6)
    add_shape = shape((2 * step + D // CHUNKS, w), BF16)
    if direct:
        mixed_x = [swap(mix_own, "head"), swap(mix_rep, "head")]
        got_q = scatter_over_seq(pack_q)
        late = after(where, k_far, got_q)
        (sum_q,) = call(add_chunks_kernel, [add_shape], got_q, [where])
        all_q = gather_over_seq(sum_q)
    else:
        mixed_x = []
        late = where
        sums = lax.psum(pack_q.astype(F32), "seq").astype(BF16)
        all_q = [sums[i] for i in range(CHUNKS)]
    (k_last,) = call(functools.partial(key_kernel, True), [acc_shape], [kv, qa_odd], [late], us=6)
    last = after(where, k_last, mixed_x, all_q)

    gn_own, gn_oth, gp_kv, share = call(
        grad_normed_kernel,
        [shape((BLOCK, D), BF16), shape((BLOCK, D), BF16), shape((rows2, 2 * w), BF16), shape((1, D), F32)],
        [events, ev_oth, inv, slope_kv, gp_gq, w4, k_own, k_far, k_last],
        [last],
    )
    (pack_kv,) = call(
        key_weights_kernel, [shape((CHUNKS, 2 * step + GAIN_ROWS, w), BF16)], [normed_t, gp_kv, share]
    )
    got_kv = scatter_over_seq(pack_kv) if direct else []
    (gn_blk,) = call(add_cores_kernel, [shape((BLOCK, D), BF16)], [gn_own, swap(gn_oth, "rep")], [where])
    if n_head == 2:
        gn_x = swap(gn_blk, "head")
        (output,) = call(
            output_kernel,
            [shape((BLOCK, D), BF16)],
            [mix_own, mix_rep, *(mixed_x or [swap(mix_own, "head"), swap(mix_rep, "head")]), out_weight, ow_x],
            [where],
            us=5,
        )
    else:
        weight = jnp.where(rep == 0, out_weight, jnp.roll(out_weight, w, axis=0))
        mixed = jnp.concatenate([mix_own, mix_rep], axis=1)
        output = lax.psum(dot_nn(mixed, weight), "head").astype(BF16)
        gn_blk = lax.psum(gn_blk.astype(F32), "head")
        gn_x = jnp.zeros_like(gn_blk)
    cat_q = jnp.concatenate(all_q, axis=0)
    grad_in, grad_out = assemble(where, [cat_q, swap(cat_q, "rep")], w)
    if direct:
        sum_kv, pg = call(
            add_chunks_gain_kernel,
            [shape((2 * step, w), BF16), shape((1, D), F32)],
            got_kv,
            [after(where, grad_out)],
        )
        pg_x = swap(pg, "head")
        all_kv = gather_over_seq(sum_kv)
    else:
        sums = lax.psum(pack_kv.astype(F32), "seq")
        all_kv = [sums[i, : 2 * step].astype(BF16) for i in range(CHUNKS)]
        pg = sums[0, 2 * step :]
        pg = lax.psum((pg[: D // w] + pg[D // w : 2 * (D // w)]).reshape(1, D), "head")
        pg_x = jnp.zeros_like(pg)
    grad_events, pg = call(
        events_kernel,
        [shape((BLOCK, D), F32), shape((1, D), F32)],
        [events, gain, gn_blk, gn_x, pg, pg_x],
        [after(where, output)],
    )
    all_kv = after(all_kv, pg)
    oth_kv = [swap(piece, "rep") for piece in all_kv]
    grad_in, pg = assemble(where, [*all_kv, *oth_kv, pg, swap(pg, "rep")], w, grad_in)
    return (output, grad_events, grad_in, grad_out, pg.reshape(D))


def assemble(where, pieces, w, grad_in=None):
    held = [] if grad_in is None else [grad_in]
    hbm, vmem = pl.BlockSpec(memory_space=pltpu.HBM), pl.BlockSpec(memory_space=pltpu.VMEM)
    return pl.pallas_call(
        functools.partial(assemble_kernel, 2 * len(held)),
        out_shape=[shape((D, 4, 2 * w), F32), shape((1, D) if held else (2 * w, D), F32)],
        in_specs=[pl.BlockSpec(memory_space=pltpu.SMEM)] + [vmem] * len(pieces) + [hbm] * len(held),
        out_specs=[hbm, vmem],
        input_output_aliases={1 + len(pieces): 0} if held else {},
        scratch_shapes=[pltpu.VMEM((2, D, 2 * w), F32), pltpu.SemaphoreType.DMA((CHUNKS, 2))],
        compiler_params=pltpu.CompilerParams(vmem_limit_bytes=VMEM_BYTES),
        cost_estimate=pl.CostEstimate(flops=0, bytes_accessed=0, transcendentals=0),
    )(where, *pieces, *held)


def solution(mesh):
    return jax.shard_map(
        body,
        mesh=mesh,
        in_specs=(
            P(("grp", "seq", "rep"), None),
            P(),
            P(None, None, "head"),
            P("head", None),
            P(("grp", "seq", "rep"), None),
            P(("grp", "seq", "rep"), None),
        ),
        out_specs=(
            P(("grp", "seq", "rep"), None),
            P(("grp", "seq", "rep"), None),
            P("grp", None, "head"),
            P(("grp", "head"), None),
            P("grp"),
        ),
        check_vma=False,
    )
```

```python
import functools

import jax
import jax.numpy as jnp
from jax import lax
from jax.experimental import pallas as pl
from jax.experimental.pallas import tpu as pltpu
from jax.sharding import PartitionSpec as P

D = 512
E = 64
BLOCK = 512
CHUNKS = 4
MASK_ROWS = 16
GAIN_ROWS = 16
LANES = 128
F32 = jnp.float32
BF16 = jnp.bfloat16
VMEM_BYTES = 16 * 1024 * 1024


def dot_nt(a, b):
    return lax.dot_general(a, b, (((1,), (1,)), ((), ())), preferred_element_type=F32)


def dot_tn(a, b):
    return lax.dot_general(a, b, (((0,), (0,)), ((), ())), preferred_element_type=F32)


def dot_nn(a, b):
    return lax.dot_general(a, b, (((1,), (0,)), ((), ())), preferred_element_type=F32)


def sigmoid(x):
    return 0.5 * jnp.tanh(0.5 * x) + 0.5


def whole(shape):
    zeros = (0,) * len(shape)
    return pl.BlockSpec(shape, lambda *_: zeros)


def call(kernel, out_shapes, args, scalars=(), us=0.0, fetched=0):
    n_scalars, n_out = len(scalars), len(out_shapes)

    def with_fetch(*refs):
        head, held, rest = refs[:n_scalars], refs[n_scalars : n_scalars + fetched], refs[n_scalars + fetched :]
        n_rest = len(args) - fetched + n_out
        slots, sems = rest[n_rest : n_rest + fetched], rest[n_rest + fetched]
        copies = [pltpu.make_async_copy(h, slot, sems.at[i]) for i, (h, slot) in enumerate(zip(held, slots))]
        for copy in copies:
            copy.start()

        def fetch(*which):
            for i in which:
                copies[i].wait()

        kernel(*head, *slots, *rest[:n_rest], fetch)

    scratch = [pltpu.VMEM(a.shape, a.dtype) for a in args[:fetched]]
    return pl.pallas_call(
        with_fetch if fetched else kernel,
        out_shape=out_shapes,
        in_specs=[pl.BlockSpec(memory_space=pltpu.SMEM)] * n_scalars
        + [pl.BlockSpec(memory_space=pltpu.HBM)] * fetched
        + [pl.BlockSpec(memory_space=pltpu.VMEM)] * (len(args) - fetched),
        out_specs=[pl.BlockSpec(memory_space=pltpu.VMEM)] * n_out,
        scratch_shapes=scratch + [pltpu.SemaphoreType.DMA((fetched,))] if fetched else [],
        compiler_params=pltpu.CompilerParams(vmem_limit_bytes=VMEM_BYTES),
        cost_estimate=pl.CostEstimate(flops=int(us * 1.1e9), bytes_accessed=0, transcendentals=0),
    )(*scalars, *args)


def shape(dims, dtype):
    return jax.ShapeDtypeStruct(dims, dtype)


def mask_at(where, mask_own, mask_oth, slot, col):
    at = jnp.where(where[1] == 1, col, 3 - col)
    return jnp.where(where[0] == slot, mask_own[0, at], mask_oth[0, at])


def slots(where):
    mine = where[0]
    return [pl.ds(pl.multiple_of(slot * BLOCK, BLOCK), BLOCK) for slot in (mine, 1 - mine)]


def project_kv_kernel(where, ev_own, ev_oth, w4, gain, normed, inv, slope, kv, fetch):
    fetch(0, 2)
    w_kv = jnp.concatenate([w4[2], w4[3]], axis=1)
    for i, (rows, events) in enumerate(zip(slots(where), (ev_own, ev_oth))):
        if i == 1:
            fetch(1)
        x = events[...].astype(F32)
        inverse = lax.rsqrt(jnp.mean(x * x, axis=1, keepdims=True) + 1e-06)
        n = (x * inverse * gain[...]).astype(BF16)
        normed[rows, :] = n
        inv[rows, :] = jnp.broadcast_to(inverse, (BLOCK, LANES))
        p = dot_nn(n, w_kv)
        s = sigmoid(p)
        slope[rows, :] = s * (1.0 + p * (1.0 - s))
        kv[rows, :] = (p * s).astype(BF16)


def project_gq_kernel(where, mask_own, mask_oth, cot_own, cot_oth, w4, ow, normed, slope, qa, gate, gm, fetch):
    w = w4.shape[2]
    fetch(0, 2, 3)
    w_gq = jnp.concatenate([w4[0], w4[1]], axis=1)
    wow = ow[pl.ds(pl.multiple_of(where[3] * w, w), w), :]
    for i, (rows, cot) in enumerate(zip(slots(where), (cot_own, cot_oth))):
        if i == 1:
            fetch(1)
        p = dot_nn(normed[rows, :], w_gq)
        s = sigmoid(p)
        slope[rows, :] = s * (1.0 + p * (1.0 - s))
        act = (p * s).astype(BF16)
        g = act[:, :w]
        gate[rows, :] = g
        grad_mixed = dot_nt(cot[...], wow)
        gm[rows, :] = grad_mixed
        qa[rows, :w] = act[:, w:]
        qa[rows, w:] = (grad_mixed * g.astype(F32)).astype(BF16)
    lane = lax.broadcasted_iota(jnp.int32, (MASK_ROWS, 2 * w), 1)
    marks = jnp.zeros((MASK_ROWS, 2 * w), F32)
    for slot in range(2):
        for col in range(4):
            m = mask_at(where, mask_own, mask_oth, slot, col).astype(F32)
            marks = jnp.where(lane == 4 * slot + col, m, marks)
    qa[2 * BLOCK :, :] = marks.astype(BF16)


TILE = 512


def block_rows(slot):
    return pl.ds(pl.multiple_of(slot * BLOCK, BLOCK), BLOCK)


def pair_side(left, l_slot, right, r_slot, acc):
    w = left.shape[1] // 2
    rows, r_rows = block_rows(l_slot), block_rows(r_slot)
    xr, yr = right[r_rows, :w], right[r_rows, w:]
    lane = lax.broadcasted_iota(jnp.int32, (1, w), 1) // E
    zero = jnp.zeros_like(xr)
    x = left[rows, :w] * jnp.asarray(0.5, BF16)
    y = left[rows, w:]
    acc_x = acc[rows, :w]
    acc_y = acc[rows, w:]
    for h in range(w // E):
        on = lane == h
        xh, yh = jnp.where(on, xr, zero), jnp.where(on, yr, zero)
        u = dot_nt(x, xh)
        g = dot_nt(y, yh)
        t = jnp.tanh(u)
        a = 1.0 + t
        m = (u * a).astype(BF16)
        slope = a.astype(BF16) + m * (1.0 - t).astype(BF16)
        acc_y = acc_y + dot_nn(m, yh)
        acc_x = acc_x + dot_nn(g.astype(BF16) * slope, xh)
    acc[rows, :w] = acc_x
    acc[rows, w:] = acc_y


def pair_both(qa, q_slot, kv, k_slot, acc_q, acc_k):
    w = qa.shape[1] // 2
    k_rows = block_rows(k_slot)
    k, v = kv[k_rows, :w], kv[k_rows, w:]
    lane = lax.broadcasted_iota(jnp.int32, (1, w), 1) // E
    zero = jnp.zeros_like(k)
    grad_k, grad_v = acc_k[k_rows, :w], acc_k[k_rows, w:]
    for t in range(BLOCK // TILE):
        rows = pl.ds(pl.multiple_of(q_slot * BLOCK + t * TILE, TILE), TILE)
        q = qa[rows, :w] * jnp.asarray(0.5, BF16)
        ga = qa[rows, w:]
        acc_x = acc_q[rows, :w]
        acc_y = acc_q[rows, w:]
        for h in range(w // E):
            on = lane == h
            kh, vh = jnp.where(on, k, zero), jnp.where(on, v, zero)
            u = dot_nt(q, kh)
            a = 1.0 + jnp.tanh(u)
            m = u * a
            slope = a + m * (2.0 - a)
            weights = m.astype(BF16)
            grad_s = (dot_nt(ga, vh) * slope).astype(BF16)
            acc_y = acc_y + dot_nn(weights, vh)
            acc_x = acc_x + dot_nn(grad_s, kh)
            grad_k = grad_k + 2.0 * dot_tn(grad_s, jnp.where(on, q, jnp.zeros_like(q)))
            grad_v = grad_v + dot_tn(weights, jnp.where(on, ga, jnp.zeros_like(ga)))
        acc_q[rows, :w] = acc_x
        acc_q[rows, w:] = acc_y
    acc_k[k_rows, :w] = grad_k
    acc_k[k_rows, w:] = grad_v


def remote_pair(t, odd):
    q_slot, k_slot = (t == 1).astype(jnp.int32), (t == 2).astype(jnp.int32)
    col = 2 + (t > 0).astype(jnp.int32)
    return (1 - q_slot, 1 - k_slot, 3 - col) if odd else (q_slot, k_slot, col)


def loop(count, step):
    lax.fori_loop(0, count, lambda t, _: (step(t), 0)[1], 0)


def query_kernel(odd, where, mask_own, mask_oth, qa, kv, acc):
    acc[...] = jnp.zeros_like(acc)

    def step(t):
        q_slot, k_slot, col = remote_pair(t, odd)

        @pl.when(mask_at(where, mask_own, mask_oth, q_slot, col) == 1)
        def _():
            pair_side(qa, q_slot, kv, k_slot, acc)

    loop(3, step)


def key_kernel(odd, where, kv, qa, acc):
    acc[...] = jnp.zeros_like(acc)
    marks = qa[2 * BLOCK :, :].astype(F32)
    row = lax.broadcasted_iota(jnp.int32, marks.shape, 0)
    lane = lax.broadcasted_iota(jnp.int32, marks.shape, 1)

    def step(t):
        q_slot, k_slot, col = remote_pair(t, odd)
        m = jnp.sum(jnp.where((row == 0) & (lane == 4 * q_slot + col), marks, 0.0))
        on = m > 0.5
        if odd:
            on = on & (where[2] == 0)

        @pl.when(on)
        def _():
            pair_side(kv, k_slot, qa, q_slot, acc)

    loop(3, step)


def own_kernel(where, mask_own, mask_oth, qa, kv, normed, acc_q, acc_k, normed_t):
    normed_t[...] = normed[...].T
    acc_q[...] = jnp.zeros_like(acc_q)
    acc_k[...] = jnp.zeros_like(acc_k)

    def step(t):
        q_slot = t % 2
        k_slot = ((t == 1) | (t == 2)).astype(jnp.int32)
        masked = mask_at(where, mask_own, mask_oth, q_slot, jnp.maximum(t - 1, 0))

        @pl.when((t < 2) | (masked == 1))
        def _():
            pair_both(qa, q_slot, kv, k_slot, acc_q, acc_k)

    loop(4, step)


def query_finish_kernel(where, cot_own, cot_oth, gate, gm, slopes, normed_t, acc_a, acc_b, acc_c, mix_own, mix_oth, gp, packed):
    w = gate.shape[1]
    grad_out = jnp.zeros((w, D), F32)
    for rows, cot, mixed in zip(slots(where), (cot_own, cot_oth), (mix_own, mix_oth)):
        total = acc_a[rows, :] + acc_b[rows, :] + acc_c[rows, :]
        grad_query = total[:, :w] * (1.0 / 1024)
        attended = total[:, w:] * (1.0 / 512)
        mix = (attended * gate[rows, :].astype(F32)).astype(BF16)
        mixed[...] = mix
        slope = slopes[rows, :]
        gp[rows, :w] = (gm[rows, :] * attended * slope[:, :w]).astype(BF16)
        gp[rows, w:] = (grad_query * slope[:, w:]).astype(BF16)
        grad_out = grad_out + dot_tn(mix, cot[...])
    pack(packed, dot_nn(normed_t[...], gp[...]), grad_out)


def pack(packed, grad_in, grad_out=None):
    step = D // CHUNKS
    w = grad_in.shape[1] // 2
    for c in range(CHUNKS):
        for p in range(2):
            packed[c, p * step : (p + 1) * step, :] = grad_in[c * step : (c + 1) * step, p * w : (p + 1) * w].astype(BF16)
        if grad_out is not None:
            n = w // CHUNKS
            part = grad_out[c * n : (c + 1) * n].astype(BF16)
            for j in range(D // w):
                packed[c, 2 * step + j * n : 2 * step + (j + 1) * n, :] = part[:, j * w : (j + 1) * w]


def grad_normed_kernel(
    where, ev_own, ev_oth, inv, slopes, gp_gq, w4, acc_a, acc_b, acc_c, gn_own, gn_oth, gp, gain
):
    w = slopes.shape[1] // 2
    w_gq = jnp.concatenate([w4[0], w4[1]], axis=1)
    w_kv = jnp.concatenate([w4[2], w4[3]], axis=1)
    share = jnp.zeros((1, D), F32)
    for rows, events, out in zip(slots(where), (ev_own, ev_oth), (gn_own, gn_oth)):
        total = acc_a[rows, :] + acc_b[rows, :] + acc_c[rows, :]
        slope = slopes[rows, :]
        gp[rows, :w] = (total[:, :w] * (1.0 / 1024) * slope[:, :w]).astype(BF16)
        gp[rows, w:] = (total[:, w:] * (1.0 / 512) * slope[:, w:]).astype(BF16)
        gn = dot_nt(gp_gq[rows, :], w_gq) + dot_nt(gp[rows, :], w_kv)
        out[...] = gn.astype(BF16)
        inverse = jnp.concatenate([inv[rows, :]] * (D // LANES), axis=1)
        share = share + jnp.sum(gn * events[...].astype(F32) * inverse, axis=0, keepdims=True)
    gain[...] = share


def key_weights_kernel(normed_t, gp, gain, packed):
    w = gp.shape[1] // 2
    pack(packed, dot_nn(normed_t[...], gp[...]))
    share = gain[...]
    high = share.astype(BF16).astype(F32)
    parts = [v[:, j * w : (j + 1) * w] for v in (high, share - high) for j in range(D // w)]
    if len(parts) < GAIN_ROWS:
        parts.append(jnp.zeros((GAIN_ROWS - len(parts), w), F32))
    for c in range(CHUNKS):
        packed[c, D // CHUNKS * 2 :, :] = jnp.concatenate(parts, axis=0).astype(BF16)


def add_cores_kernel(order, a, b, out):
    out[...] = (a[...].astype(F32) + b[...].astype(F32)).astype(BF16)


def add_chunks_gain_kernel(order, *refs):
    pieces, (out, gain) = refs[:4], refs[4:]
    n, w = out.shape
    a, b, c, d = (piece[...].astype(F32) for piece in pieces)
    total = (a + b) + (c + d)
    out[...] = total[:n].astype(BF16)
    k = D // w
    for j in range(k):
        gain[:, j * w : (j + 1) * w] = total[n + j : n + j + 1] + total[n + k + j : n + k + j + 1]


def add_chunks_kernel(order, a, b, c, d, out):
    out[...] = ((a[...].astype(F32) + b[...].astype(F32)) + (c[...].astype(F32) + d[...].astype(F32))).astype(BF16)


def assemble_kernel(first, where, *refs):
    if first:
        pieces, (pg_a, pg_b, _, grad_in, pg, parts, sem) = refs[:8], refs[8:]
        pg[...] = pg_a[...] + pg_b[...]
    else:
        both, (grad_in, grad_out, parts, sem) = refs[:2], refs[2:]
        n = both[0].shape[0] // CHUNKS
        pieces = [held.at[pl.ds(i * n, n)] for held in both for i in range(CHUNKS)]
    w = pieces[0].shape[1]
    step = D // CHUNKS
    n = w // CHUNKS

    def place(i, piece, core):
        lanes = slice(core * w, (core + 1) * w)
        rows = pl.ds(pl.multiple_of(where[4 + i] * step, step), step)
        for p in range(2):
            parts[p, rows, lanes] = piece[p * step : (p + 1) * step, :].astype(F32)
        if first == 0:
            for j in range(D // w):
                block = piece[2 * step + j * n : 2 * step + (j + 1) * n, :]
                out_rows = pl.ds(pl.multiple_of(core * w + where[4 + i] * n, n), n)
                grad_out[out_rows, j * w : (j + 1) * w] = block.astype(F32)

    def copy(i, p):
        rows = pl.ds(pl.multiple_of(where[4 + i] * step, step), step)
        return pltpu.make_async_copy(parts.at[p, rows], grad_in.at[rows, first + p], sem.at[i, p])

    for i in range(CHUNKS):
        for core in range(2):

            @pl.when(where[3] == core)
            def _():
                place(i, pieces[i], core)
                place(i, pieces[4 + i], 1 - core)

        for p in range(2):
            copy(i, p).start()
    for i in range(CHUNKS):
        for p in range(2):
            copy(i, p).wait()


def events_kernel(order, events, gain, mine, other, pg_a, pg_b, grad, pg):
    x = events[...].astype(F32)
    inverse = lax.rsqrt(jnp.mean(x * x, axis=1, keepdims=True) + 1e-06)
    gn = mine[...].astype(F32) + other[...].astype(F32)
    scaled = gn * gain[...]
    mean = jnp.mean(scaled * x, axis=1, keepdims=True)
    grad[...] = inverse * scaled - x * (inverse * inverse * inverse) * mean
    pg[...] = pg_a[...] + pg_b[...]


def output_kernel(where, mine, rep, mine_x, rep_x, ow, ow_x, out):
    w = mine.shape[1]
    r = where[3]
    first = pl.ds(pl.multiple_of(r * w, w), w)
    second = pl.ds(pl.multiple_of((1 - r) * w, w), w)
    here = dot_nn(mine[...], ow[first, :]) + dot_nn(rep[...], ow[second, :])
    there = dot_nn(mine_x[...], ow_x[first, :]) + dot_nn(rep_x[...], ow_x[second, :])
    out[...] = (here + there).astype(BF16)


def swap(x, axis, bit=1):
    n = lax.axis_size(axis)
    return lax.ppermute(x, axis, [(i, i ^ bit) for i in range(n)])


def route_even(n):
    return [(2 * i + r, 2 * (i ^ 1) + r) for i in range(n) for r in range(2)]


def route_odd(n):
    route = []
    for i in range(n):
        for r in range(2):
            if i in (0, n - 1):
                route.append((2 * i + r, 2 * i + 1 - r))
            else:
                route.append((2 * i + r, 2 * (((i - 1) ^ 1) + 1) + r))
    return route


def scatter_over_seq(packed):
    me = lax.axis_index("seq")

    def chunk(d):
        return lax.dynamic_index_in_dim(packed, me ^ d, 0, keepdims=False)

    return [chunk(0)] + [swap(chunk(d), "seq", d) for d in (1, 2, 3)]


def gather_over_seq(total):
    return [total] + [swap(total, "seq", d) for d in (1, 2, 3)]


def after(values, *others):
    return lax.optimization_barrier((values, others))[0]


def body(events, norm_gain, in_weight, out_weight, pair_mask, cotangent):
    n_seq, n_head = lax.axis_size("seq"), lax.axis_size("head")
    direct = n_seq == CHUNKS and n_head == 2
    rep, seq = lax.axis_index("rep"), lax.axis_index("seq")
    w = in_weight.shape[2] // 2
    rows2 = 2 * BLOCK
    step = D // CHUNKS
    flip = 1 - seq % 2
    edge = ((seq == 0) | (seq == n_seq - 1)).astype(jnp.int32)
    chunk_ids = [(seq ^ d) if direct else jnp.int32(d) for d in range(CHUNKS)]
    where = jnp.stack([rep ^ flip, flip, edge, rep] + chunk_ids).astype(jnp.int32)

    ev_oth = swap(events, "rep")
    cot_oth = swap(cotangent, "rep")
    mask_oth = swap(pair_mask, "rep")
    scalars = [where, pair_mask, mask_oth]
    gain = norm_gain.reshape(1, D)
    w4 = lax.dynamic_slice(in_weight, (0, 0, rep * w), (D, 4, w)).transpose(1, 0, 2)
    axes = ("seq", "rep")
    even, odd = route_even(n_seq), route_odd(n_seq)

    normed, inv, slope_kv, kv = call(
        project_kv_kernel,
        [shape((rows2, D), BF16), shape((rows2, LANES), F32), shape((rows2, 2 * w), F32), shape((rows2, 2 * w), BF16)],
        [events, ev_oth, w4, gain],
        [where],
        fetched=3,
    )
    kv_even = lax.ppermute(kv, axes, even)
    kv_odd = lax.ppermute(kv, axes, odd)
    slope_gq, qa, gate, gm = call(
        project_gq_kernel,
        [
            shape((rows2, 2 * w), F32),
            shape((rows2 + MASK_ROWS, 2 * w), BF16),
            shape((rows2, w), BF16),
            shape((rows2, w), F32),
        ],
        [cotangent, cot_oth, w4, out_weight, normed],
        scalars,
        fetched=4,
    )
    qa_even = lax.ppermute(qa, axes, even)
    qa_odd = lax.ppermute(qa, axes, odd)
    acc_shape = shape((rows2, 2 * w), F32)
    q_own, k_own, normed_t = call(
        own_kernel, [acc_shape, acc_shape, shape((D, rows2), BF16)], [qa, kv, normed], scalars, us=9
    )
    (q_even,) = call(functools.partial(query_kernel, False), [acc_shape], [qa, kv_even], scalars, us=5)
    late = where
    if n_head == 2:
        ow_x = swap(out_weight, "head")
        late = after(where, ow_x, q_even)
    (q_odd,) = call(
        functools.partial(query_kernel, True), [acc_shape], [qa, kv_odd], [late, pair_mask, mask_oth], us=5
    )
    mix_own, mix_oth, gp_gq, pack_q = call(
        query_finish_kernel,
        [
            shape((BLOCK, w), BF16),
            shape((BLOCK, w), BF16),
            shape((rows2, 2 * w), BF16),
            shape((CHUNKS, 2 * step + D // CHUNKS, w), BF16),
        ],
        [cotangent, cot_oth, gate, gm, slope_gq, normed_t, q_own, q_even, q_odd],
        [where],
    )
    mix_rep = swap(mix_oth, "rep")
    (k_far,) = call(functools.partial(key_kernel, False), [acc_shape], [kv, qa_even], [where], us=6)
    add_shape = shape((2 * step + D // CHUNKS, w), BF16)
    if direct:
        mixed_x = [swap(mix_own, "head"), swap(mix_rep, "head")]
        got_q = scatter_over_seq(pack_q)
        late = after(where, k_far, got_q)
        (sum_q,) = call(add_chunks_kernel, [add_shape], got_q, [where])
        all_q = gather_over_seq(sum_q)
    else:
        mixed_x = []
        late = where
        sums = lax.psum(pack_q.astype(F32), "seq").astype(BF16)
        all_q = [sums[i] for i in range(CHUNKS)]
    (k_last,) = call(functools.partial(key_kernel, True), [acc_shape], [kv, qa_odd], [late], us=6)
    last = after(where, k_last, mixed_x, all_q)

    gn_own, gn_oth, gp_kv, share = call(
        grad_normed_kernel,
        [shape((BLOCK, D), BF16), shape((BLOCK, D), BF16), shape((rows2, 2 * w), BF16), shape((1, D), F32)],
        [events, ev_oth, inv, slope_kv, gp_gq, w4, k_own, k_far, k_last],
        [last],
    )
    (pack_kv,) = call(
        key_weights_kernel, [shape((CHUNKS, 2 * step + GAIN_ROWS, w), BF16)], [normed_t, gp_kv, share]
    )
    got_kv = scatter_over_seq(pack_kv) if direct else []
    (gn_blk,) = call(add_cores_kernel, [shape((BLOCK, D), BF16)], [gn_own, swap(gn_oth, "rep")], [where])
    if n_head == 2:
        gn_x = swap(gn_blk, "head")
        (output,) = call(
            output_kernel,
            [shape((BLOCK, D), BF16)],
            [mix_own, mix_rep, *(mixed_x or [swap(mix_own, "head"), swap(mix_rep, "head")]), out_weight, ow_x],
            [where],
            us=5,
        )
    else:
        weight = jnp.where(rep == 0, out_weight, jnp.roll(out_weight, w, axis=0))
        mixed = jnp.concatenate([mix_own, mix_rep], axis=1)
        output = lax.psum(dot_nn(mixed, weight), "head").astype(BF16)
        gn_blk = lax.psum(gn_blk.astype(F32), "head")
        gn_x = jnp.zeros_like(gn_blk)
    cat_q = jnp.concatenate(all_q, axis=0)
    grad_in, grad_out = assemble(where, [cat_q, swap(cat_q, "rep")], w)
    if direct:
        sum_kv, pg = call(
            add_chunks_gain_kernel,
            [shape((2 * step, w), BF16), shape((1, D), F32)],
            got_kv,
            [after(where, grad_out)],
        )
        pg_x = swap(pg, "head")
        all_kv = gather_over_seq(sum_kv)
    else:
        sums = lax.psum(pack_kv.astype(F32), "seq")
        all_kv = [sums[i, : 2 * step].astype(BF16) for i in range(CHUNKS)]
        pg = sums[0, 2 * step :]
        pg = lax.psum((pg[: D // w] + pg[D // w : 2 * (D // w)]).reshape(1, D), "head")
        pg_x = jnp.zeros_like(pg)
    grad_events, pg = call(
        events_kernel,
        [shape((BLOCK, D), F32), shape((1, D), F32)],
        [events, gain, gn_blk, gn_x, pg, pg_x],
        [after(where, output)],
    )
    all_kv = after(all_kv, pg)
    oth_kv = [swap(piece, "rep") for piece in all_kv]
    grad_in, pg = assemble(where, [*all_kv, *oth_kv, pg, swap(pg, "rep")], w, grad_in)
    return (output, grad_events, grad_in, grad_out, pg.reshape(D))


def assemble(where, pieces, w, grad_in=None):
    held = [] if grad_in is None else [grad_in]
    hbm, vmem = pl.BlockSpec(memory_space=pltpu.HBM), pl.BlockSpec(memory_space=pltpu.VMEM)
    return pl.pallas_call(
        functools.partial(assemble_kernel, 2 * len(held)),
        out_shape=[shape((D, 4, 2 * w), F32), shape((1, D) if held else (2 * w, D), F32)],
        in_specs=[pl.BlockSpec(memory_space=pltpu.SMEM)] + [vmem] * len(pieces) + [hbm] * len(held),
        out_specs=[hbm, vmem],
        input_output_aliases={1 + len(pieces): 0} if held else {},
        scratch_shapes=[pltpu.VMEM((2, D, 2 * w), F32), pltpu.SemaphoreType.DMA((CHUNKS, 2))],
        compiler_params=pltpu.CompilerParams(vmem_limit_bytes=VMEM_BYTES),
        cost_estimate=pl.CostEstimate(flops=0, bytes_accessed=0, transcendentals=0),
    )(where, *pieces, *held)


def solution(mesh):
    return jax.shard_map(
        body,
        mesh=mesh,
        in_specs=(
            P(("grp", "seq", "rep"), None),
            P(),
            P(None, None, "head"),
            P("head", None),
            P(("grp", "seq", "rep"), None),
            P(("grp", "seq", "rep"), None),
        ),
        out_specs=(
            P(("grp", "seq", "rep"), None),
            P(("grp", "seq", "rep"), None),
            P("grp", None, "head"),
            P(("grp", "head"), None),
            P("grp"),
        ),
        check_vma=False,
    )
```
